32 devices in a mesh: gx: 4 (over z), gy: 8 (over y, x, core).
Axes of the slice: x: 2, y: 2, z: 4, core: 2. Of those that a mesh axis runs over, the one named last changes fastest.
Arguments:
- hidden_in: bfloat16 [32, 8192], P(('gx', 'gy')), may hold values from -6 to 6
- norm_gain: float32 [8192], replicated, may hold values from 0.5 to 1.5
- w_query: bfloat16 [8192, 8192], P('gx', 'gy'), may hold values from -0.0625 to 0.0625
- key_weight: bfloat16 [8192, 1024], P('gx', 'gy'), may hold values from -0.375 to 0.375
- value_weight: bfloat16 [8192, 1024], P('gx', 'gy'), may hold values from -0.0625 to 0.0625
- w_output: bfloat16 [8192, 8192], P('gx', 'gy'), may hold values from -0.0625 to 0.0625
- key_cache_units: bfloat16 [32, 2048, 1024], P(('gx', 'gy')), may hold values from -6 to 6
- value_cache_units: bfloat16 [32, 2048, 1024], P(('gx', 'gy')), may hold values from -6 to 6
- key_scale: float32 [32, 16, 8], P(('gx', 'gy')), may hold values from 0.5 to 40
- value_block_scale: float32 [32, 16, 8], P(('gx', 'gy')), may hold values from 0.5 to 2
- lengths: int32 [32], P(('gx', 'gy')), may hold values from 256 to 2048, as said below
Outputs:
- hidden_out: bfloat16 [32, 8192], P(('gx', 'gy'))
The draws below stay inside these ranges and needn't reach their ends.
Inputs may be any that keep to these rules, and one draw needn't show every extreme that they name: Request r has lengths[r] cached tokens at positions 0 to lengths[r] - 1 of its cache, the new token stands at position lengths[r]; some request has exactly 2048 and some exactly 256.
All inputs are finite; a program needn't handle non-finite values.
Results may differ from the reference program's by a relative error of at most 0.008.
The reference program's roundings to bfloat16 on the way count: a program that leaves them out, or rounds other values in their place, can miss the bound.
Values may be sent and summed in bfloat16 or wider, within the bound.
No kernel may reach another device: no remote copies, remote signals or barrier semaphores. Data moves between devices by JAX's collectives and lax.ppermute only.
A program may use at most 64 MiB of HBM per device.

```python
import math
import jax
import jax.numpy as jnp
from jax import lax

MODEL_WIDTH = 8192
HQ = 64
KEY_VALUE_HEADS = 8
HEAD_SIZE = 128
CACHE_SLOTS = 2048
SCALE_BLOCK = 128
REQUEST_COUNT = 32


def draw_key_scale(key, part):
    key_base = jax.random.fold_in(key, 0)
    scale_layout = (REQUEST_COUNT, CACHE_SLOTS // SCALE_BLOCK, KEY_VALUE_HEADS)
    scales = jnp.exp(jax.random.uniform(key_base, scale_layout, jnp.float32, math.log(0.5), math.log(5.0)))
    return scales


def draw_lengths(key, part):
    key_vals, key_long, key_short = jax.random.split(key, 3)
    sampled = jax.random.randint(key_vals, (REQUEST_COUNT,), CACHE_SLOTS // 8, CACHE_SLOTS + 1)
    long_place = jax.random.randint(key_long, (), 0, REQUEST_COUNT)
    short_step = jax.random.randint(key_short, (), 1, REQUEST_COUNT)
    short_place = (long_place + short_step) % REQUEST_COUNT
    sampled = sampled.at[long_place].set(CACHE_SLOTS)
    return sampled.at[short_place].set(CACHE_SLOTS // 8)


def level_of(stream_key, shape, cuts, least, top_value):
    level, own = 1.0, jax.random.fold_in(stream_key, 6)
    for dim, parts in cuts:
        heights = jnp.exp(jax.random.uniform(jax.random.fold_in(own, dim), (parts,), jnp.float32, least / len(cuts), top_value / len(cuts)))
        level = level * jnp.repeat(heights, shape[dim] // parts).reshape([-1 if axis == dim else 1 for axis in range(len(shape))])
    return level


def gaussian(own_key, extent, scale, bound, cuts=(), kind=jnp.bfloat16):
    drawn = jax.random.normal(own_key, extent, jnp.float32) * scale
    if len(cuts) > 0:
        drawn = level_of(own_key, extent, cuts, -0.22, 0.18) * drawn
    return jnp.clip(drawn, min=-bound, max=bound).astype(kind)


def setup_inputs(seed: int = 0) -> dict:
    seeds = jax.random.split(jax.random.key(seed), 12)
    hidden_in = gaussian(seeds[0], (REQUEST_COUNT, MODEL_WIDTH), 1.0, 6.0, ((0, 32),))
    norm_gain = jnp.clip(1.0 + 0.1 * jax.random.normal(seeds[1], (MODEL_WIDTH,), jnp.float32), 0.5, 1.5)
    w_query = gaussian(seeds[2], (MODEL_WIDTH, HQ * HEAD_SIZE), MODEL_WIDTH ** -0.5, 0.0625, ((0, 4), (1, 8)))
    key_weight = gaussian(seeds[3], (MODEL_WIDTH, KEY_VALUE_HEADS * HEAD_SIZE), (MODEL_WIDTH // 32) ** -0.5, 0.375, ((0, 4), (1, 8)))
    value_weight = gaussian(seeds[4], (MODEL_WIDTH, KEY_VALUE_HEADS * HEAD_SIZE), MODEL_WIDTH ** -0.5, 0.0625, ((0, 4), (1, 8)))
    w_output = gaussian(seeds[5], (HQ * HEAD_SIZE, MODEL_WIDTH), (HQ * HEAD_SIZE) ** -0.5, 0.0625, ((0, 4), (1, 8)))
    key_cache_units = gaussian(seeds[6], (REQUEST_COUNT, CACHE_SLOTS, KEY_VALUE_HEADS * HEAD_SIZE), 1.0, 6.0, ((0, 32),))
    value_cache_units = gaussian(seeds[7], (REQUEST_COUNT, CACHE_SLOTS, KEY_VALUE_HEADS * HEAD_SIZE), 1.0, 6.0, ((0, 32),))
    key_scale = draw_key_scale(jax.random.fold_in(seeds[11], 71), 0)
    value_block_scale = jnp.clip(jnp.exp(math.log(2.0) - 1.3862944 * jax.random.uniform(seeds[9], (REQUEST_COUNT, CACHE_SLOTS // SCALE_BLOCK, KEY_VALUE_HEADS), jnp.float32) ** level_of(seeds[9], (REQUEST_COUNT, CACHE_SLOTS // SCALE_BLOCK, KEY_VALUE_HEADS), ((0, 32),), -0.2, 0.2)), 0.5, 2.0)
    lengths = draw_lengths(jax.random.fold_in(seeds[11], 71), 0)
    return dict(hidden_in=hidden_in, norm_gain=norm_gain, w_query=w_query, key_weight=key_weight, value_weight=value_weight, w_output=w_output, key_cache_units=key_cache_units, value_cache_units=value_cache_units, key_scale=key_scale, value_block_scale=value_block_scale, lengths=lengths)


ROPE_BASE = 500000.0
NORM_EPS = 1e-05
MASKED_SCORE = -1e+30

def apply_rotary(values, positions):
    head_dim = values.shape[-1]
    half_dim = head_dim // 2
    freqs = ROPE_BASE ** (-(jnp.arange(half_dim, dtype=jnp.float32) * 2.0) / head_dim)
    angles = positions.astype(jnp.float32)[:, None, None] * freqs
    cosine = jnp.cos(angles)
    sine = jnp.sin(angles)
    wide_vals = values.astype(jnp.float32)
    front_half = wide_vals[..., :half_dim]
    back_half = wide_vals[..., half_dim:]
    joined = jnp.concatenate([front_half * cosine - back_half * sine, back_half * cosine + front_half * sine], axis=-1)
    return joined.astype(jnp.bfloat16)

def attend_exact(query, new_key, new_value, keys, values, key_scale, value_block_scale, length):
    heads, head_dim = query.shape
    kv_heads = new_key.shape[0]
    capacity = keys.shape[0]
    group_size = heads // kv_heads
    blocks = key_scale.shape[0]
    inv_root = 1.0 / math.sqrt(head_dim)
    grouped = query.reshape(kv_heads, group_size, head_dim).astype(jnp.float32)
    key_rows = keys.reshape(capacity, kv_heads, head_dim).astype(jnp.float32)
    value_rows = values.reshape(capacity, kv_heads, head_dim).astype(jnp.float32)
    raw_scores = jnp.einsum('gqd,tgd->gqt', grouped, key_rows)
    scaled = raw_scores.reshape(kv_heads, group_size, blocks, capacity // blocks) * key_scale.T[:, None, :, None]
    scores = scaled.reshape(kv_heads, group_size, capacity) * inv_root
    live_mask = jnp.arange(capacity) < length
    scores = jnp.where(live_mask, scores, MASKED_SCORE)
    own_score = jnp.einsum('gqd,gd->gq', grouped, new_key.astype(jnp.float32)) * inv_root
    peak_score = jnp.maximum(lax.optimization_barrier(jnp.max(scores, axis=-1)), own_score)
    probs = jnp.where(live_mask, jnp.exp(scores - peak_score[..., None]), 0.0)
    own_prob = jnp.exp(own_score - peak_score)
    total_weight = lax.optimization_barrier(jnp.sum(probs, axis=-1)) + own_prob
    scaled_probs = probs.reshape(kv_heads, group_size, blocks, capacity // blocks) * value_block_scale.T[:, None, :, None]
    weighted = lax.optimization_barrier(scaled_probs.reshape(kv_heads, group_size, capacity).astype(jnp.bfloat16)).astype(jnp.float32)
    own_weight = lax.optimization_barrier(own_prob.astype(jnp.bfloat16)).astype(jnp.float32)
    summed = jnp.einsum('gqt,tgd->gqd', weighted, value_rows)
    summed = summed + own_weight[..., None] * new_value.astype(jnp.float32)[:, None, :]
    return (summed / total_weight[..., None]).astype(jnp.bfloat16).reshape(heads * head_dim)

def reference(hidden_in, norm_gain, w_query, key_weight, value_weight, w_output, key_cache_units, value_cache_units, key_scale, value_block_scale, lengths):
    wide_input = hidden_in.astype(jnp.float32)
    variance = lax.optimization_barrier(jnp.mean(wide_input * wide_input, axis=1, keepdims=True))
    normed = (wide_input * lax.rsqrt(variance + NORM_EPS) * norm_gain).astype(jnp.bfloat16)
    query_proj = jnp.dot(normed, w_query, preferred_element_type=jnp.float32).astype(jnp.bfloat16)
    key_projected = jnp.dot(normed, key_weight, preferred_element_type=jnp.float32).astype(jnp.bfloat16)
    value_projected = jnp.dot(normed, value_weight, preferred_element_type=jnp.float32).astype(jnp.bfloat16)
    query_rot = apply_rotary(query_proj.reshape(REQUEST_COUNT, HQ, HEAD_SIZE), lengths)
    key_rotated = apply_rotary(key_projected.reshape(REQUEST_COUNT, KEY_VALUE_HEADS, HEAD_SIZE), lengths)
    fresh_value = value_projected.reshape(REQUEST_COUNT, KEY_VALUE_HEADS, HEAD_SIZE)
    attended = lax.map(lambda items: attend_exact(*items), (query_rot, key_rotated, fresh_value, key_cache_units, value_cache_units, key_scale, value_block_scale, lengths))
    update = jnp.dot(attended, w_output, preferred_element_type=jnp.float32)
    return (wide_input + update).astype(jnp.bfloat16)
```

```python
import math

import jax
import jax.numpy as jnp
from jax import lax
from jax.sharding import PartitionSpec as P

HQ = 64
KEY_VALUE_HEADS = 8
HEAD_SIZE = 128


ROPE_BASE = 500000.0
NORM_EPS = 1e-05
MASKED_SCORE = -1e30


def apply_rotary(values, positions):
    head_dim = values.shape[-1]
    half_dim = head_dim // 2
    freqs = ROPE_BASE ** (-(jnp.arange(half_dim, dtype=jnp.float32) * 2.0) / head_dim)
    angles = positions.astype(jnp.float32)[:, None, None] * freqs
    cosine = jnp.cos(angles)
    sine = jnp.sin(angles)
    wide_vals = values.astype(jnp.float32)
    front_half = wide_vals[..., :half_dim]
    back_half = wide_vals[..., half_dim:]
    joined = jnp.concatenate(
        [front_half * cosine - back_half * sine, back_half * cosine + front_half * sine], axis=-1
    )
    return joined.astype(jnp.bfloat16)


def attend(query, new_key, new_value, keys, values, key_scale, value_block_scale, length):
    heads, head_dim = query.shape
    kv_heads = new_key.shape[0]
    capacity = keys.shape[0]
    group_size = heads // kv_heads
    blocks = key_scale.shape[0]
    inv_root = 1.0 / math.sqrt(head_dim)
    grouped = query.reshape(kv_heads, group_size, head_dim)
    key_rows = keys.reshape(capacity, kv_heads, head_dim)
    value_rows = values.reshape(capacity, kv_heads, head_dim)
    raw_scores = jnp.einsum("gqd,tgd->gqt", grouped, key_rows, preferred_element_type=jnp.float32)
    scaled = (
        raw_scores.reshape(kv_heads, group_size, blocks, capacity // blocks)
        * key_scale.T[:, None, :, None]
    )
    scores = scaled.reshape(kv_heads, group_size, capacity) * inv_root
    live_mask = jnp.arange(capacity) < length
    scores = jnp.where(live_mask, scores, MASKED_SCORE)
    own_score = (
        jnp.einsum("gqd,gd->gq", grouped, new_key, preferred_element_type=jnp.float32) * inv_root
    )
    peak_score = jnp.maximum(jnp.max(scores, axis=-1), own_score)
    probs = jnp.where(live_mask, jnp.exp(scores - peak_score[..., None]), 0.0)
    own_prob = jnp.exp(own_score - peak_score)
    total_weight = jnp.sum(probs, axis=-1) + own_prob
    scaled_probs = (
        probs.reshape(kv_heads, group_size, blocks, capacity // blocks)
        * value_block_scale.T[:, None, :, None]
    )
    weighted = scaled_probs.reshape(kv_heads, group_size, capacity).astype(jnp.bfloat16)
    own_weight = lax.optimization_barrier(own_prob.astype(jnp.bfloat16)).astype(jnp.float32)
    summed = jnp.einsum("gqt,tgd->gqd", weighted, value_rows, preferred_element_type=jnp.float32)
    summed = summed + own_weight[..., None] * new_value.astype(jnp.float32)[:, None, :]
    return (summed / total_weight[..., None]).astype(jnp.bfloat16).reshape(heads * head_dim)


def exchange(blocks):
    return lax.all_to_all(blocks, ("gx", "gy"), split_axis=0, concat_axis=0, tiled=True)


def gather_slices(local_rows):
    row_groups, column_groups = lax.axis_size("gx"), lax.axis_size("gy")
    local_count, feature_count = local_rows.shape
    width = feature_count // row_groups
    blocks = local_rows.reshape(local_count, row_groups, 1, width // 128, 128).transpose(1, 2, 0, 3, 4)
    blocks = jnp.broadcast_to(blocks, (row_groups, column_groups) + blocks.shape[2:])
    blocks = blocks.reshape(-1, local_count, width // 128, 128)
    return exchange(blocks).reshape(-1, width)


def scatter_sums(partial_rows):
    row_groups, column_groups = lax.axis_size("gx"), lax.axis_size("gy")
    request_total, columns = partial_rows.shape
    devices = row_groups * column_groups
    blocks = partial_rows.reshape(devices, request_total // devices, columns // 128, 128)
    arrived = exchange(blocks).reshape(row_groups, column_groups, -1, columns)
    return jnp.sum(arrived, axis=0)


def body(
    hidden_in,
    norm_gain,
    w_query,
    key_weight,
    value_weight,
    w_output,
    key_cache_units,
    value_cache_units,
    key_scale,
    value_block_scale,
    lengths,
):
    request_rows = hidden_in.shape[0]
    wide_input = hidden_in.astype(jnp.float32)
    variance = jnp.mean(wide_input * wide_input, axis=1, keepdims=True)
    normed = (wide_input * lax.rsqrt(variance + NORM_EPS) * norm_gain).astype(jnp.bfloat16)
    query_cols = w_query.shape[1]
    key_cols = key_weight.shape[1]
    columns = gather_slices(normed)
    projected = jnp.concatenate(
        [
            jnp.dot(columns, weight, preferred_element_type=jnp.float32)
            for weight in (w_query, key_weight, value_weight)
        ],
        axis=1,
    )
    summed = scatter_sums(projected).astype(jnp.bfloat16).swapaxes(0, 1)
    query_full = summed[:, :, :query_cols]
    key_complete = summed[:, :, query_cols : query_cols + key_cols]
    value_complete = summed[:, :, query_cols + key_cols :]
    query_rot = apply_rotary(query_full.reshape(request_rows, HQ, HEAD_SIZE), lengths)
    key_rotated = apply_rotary(
        key_complete.reshape(request_rows, KEY_VALUE_HEADS, HEAD_SIZE), lengths
    )
    fresh_value = value_complete.reshape(request_rows, KEY_VALUE_HEADS, HEAD_SIZE)
    attended = jax.vmap(attend)(
        query_rot,
        key_rotated,
        fresh_value,
        key_cache_units,
        value_cache_units,
        key_scale,
        value_block_scale,
        lengths,
    )
    update_part = jnp.dot(gather_slices(attended), w_output, preferred_element_type=jnp.float32)
    update = scatter_sums(update_part).swapaxes(0, 1).reshape(request_rows, -1)
    return (wide_input + update).astype(jnp.bfloat16)


def solution(mesh):
    placed = (
        P(("gx", "gy"), None),
        P(),
        P("gx", "gy"),
        P("gx", "gy"),
        P("gx", "gy"),
        P("gx", "gy"),
        P(("gx", "gy"), None, None),
        P(("gx", "gy"), None, None),
        P(("gx", "gy"), None, None),
        P(("gx", "gy"), None, None),
        P(("gx", "gy")),
    )
    return jax.shard_map(
        body, mesh=mesh, in_specs=placed, out_specs=P(("gx", "gy"), None), check_vma=False
    )
```

```python
import functools
import math

import jax
import jax.numpy as jnp
from jax import lax
from jax.experimental import pallas as pl
from jax.experimental.pallas import tpu as pltpu
from jax.sharding import PartitionSpec as P

HQ = 64
KEY_VALUE_HEADS = 8
HEAD_SIZE = 128
GROUP = HQ // KEY_VALUE_HEADS

ROPE_BASE = 500000.0
NORM_EPS = 1e-05
MASKED_SCORE = -1e30

LANES = 128
VMEM = pl.BlockSpec(memory_space=pltpu.VMEM)
SMEM = pl.BlockSpec(memory_space=pltpu.SMEM)
PARAMS = pltpu.CompilerParams(vmem_limit_bytes=24 * 1024 * 1024)


def exchange(blocks):
    return lax.all_to_all(blocks, ("gx", "gy"), split_axis=0, concat_axis=0, tiled=True)


def in_vmem(array):
    return pltpu.with_memory_space_constraint(array, pltpu.VMEM)


def norm_kernel(row_groups, hidden_ref, gain_ref, blocks_ref, wide_ref):
    rows = wide_ref.shape[0]
    for row in range(rows):
        wide_ref[row : row + 1, :] = hidden_ref[:, row * LANES : (row + 1) * LANES].astype(
            jnp.float32
        )
    wide = wide_ref[...]
    variance = jnp.sum(wide * wide, keepdims=True) * (1.0 / (rows * LANES))
    normed = (wide * lax.rsqrt(variance + NORM_EPS) * gain_ref[...]).astype(jnp.bfloat16)
    spread_blocks(normed, row_groups, blocks_ref)


def spread_blocks(rows, row_groups, blocks_ref):
    per_block = rows.shape[0] // row_groups
    column_groups = blocks_ref.shape[0] // row_groups
    for i in range(row_groups):
        part = rows[i * per_block : (i + 1) * per_block]
        for j in range(column_groups):
            blocks_ref[i * column_groups + j] = part


def flat_rows(blocks_ref):
    return jnp.concatenate([blocks_ref[:, k, :] for k in range(blocks_ref.shape[1])], axis=1)


def send_rows(product, out_ref):
    requests, columns = product.shape
    count = columns // LANES
    for n in range(count):
        out_ref[pl.ds(n, requests, stride=count), :] = product[:, n * LANES : (n + 1) * LANES]


def project_kernel(blocks_ref, w_query_ref, key_ref, value_ref, out_ref):
    rows = flat_rows(blocks_ref)
    send_rows(
        jnp.concatenate(
            [
                jnp.dot(rows, ref[...], preferred_element_type=jnp.float32)
                for ref in (w_query_ref, key_ref, value_ref)
            ],
            axis=1,
        ),
        out_ref,
    )


def output_kernel(blocks_ref, weight_ref, out_ref):
    rows = flat_rows(blocks_ref)
    send_rows(jnp.dot(rows, weight_ref[...], preferred_element_type=jnp.float32), out_ref)


def attend_kernel(
    row_groups,
    length_ref,
    key_scale_ref,
    value_scale_ref,
    turn_ref,
    sums_ref,
    keys_ref,
    values_ref,
    blocks_ref,
    score_ref,
    result_ref,
):
    length = length_ref[0]
    capacity = keys_ref.shape[0]
    scale_blocks = key_scale_ref.shape[1]
    block = capacity // scale_blocks
    inv_root = 1.0 / math.sqrt(HEAD_SIZE)
    per_group = GROUP + 2
    cosine, sine = turn_ref[0:1, :], turn_ref[1:2, :]

    def rotate(wide):
        return (wide * cosine + pltpu.roll(wide, HEAD_SIZE // 2, 1) * sine).astype(jnp.bfloat16)

    def summed(first, count):
        total = sums_ref[first : first + count, :]
        for i in range(1, row_groups):
            start = i * KEY_VALUE_HEADS * per_group + first
            total = total + sums_ref[start : start + count, :]
        return total.astype(jnp.bfloat16).astype(jnp.float32)

    positions = lax.broadcasted_iota(jnp.int32, (1, capacity), 1)
    live = positions < length
    queries, own_scores, new_values = [], [], []
    for g in range(KEY_VALUE_HEADS):
        query = rotate(summed(g * per_group, GROUP))
        new_key = rotate(summed(g * per_group + GROUP, 1))
        new_values.append(summed(g * per_group + GROUP + 1, 1))
        own_scores.append(
            jnp.sum(
                query.astype(jnp.float32) * new_key.astype(jnp.float32), axis=1, keepdims=True
            )
            * inv_root
        )
        queries.append(query)
    for g in range(KEY_VALUE_HEADS):
        raw = lax.dot_general(
            queries[g],
            keys_ref[:, g * HEAD_SIZE : (g + 1) * HEAD_SIZE],
            (((1,), (1,)), ((), ())),
            preferred_element_type=jnp.float32,
        )
        for b in range(scale_blocks):
            span = slice(b * block, (b + 1) * block)
            scaled = raw[:, span] * key_scale_ref[g, b] * inv_root
            score_ref[g * GROUP : (g + 1) * GROUP, span] = jnp.where(
                live[:, span], scaled, MASKED_SCORE
            )
    for g in range(KEY_VALUE_HEADS):
        heads = slice(g * GROUP, (g + 1) * GROUP)
        scores = score_ref[heads, :]
        peak = jnp.maximum(jnp.max(scores, axis=1, keepdims=True), own_scores[g])
        probs = jnp.where(live, jnp.exp(scores - peak), 0.0)
        own_prob = jnp.exp(own_scores[g] - peak)
        total = jnp.sum(probs, axis=1, keepdims=True) + own_prob
        weighted = jnp.concatenate(
            [
                (probs[:, b * block : (b + 1) * block] * value_scale_ref[g, b]).astype(jnp.bfloat16)
                for b in range(scale_blocks)
            ],
            axis=1,
        )
        own_weight = own_prob.astype(jnp.bfloat16).astype(jnp.float32)
        sums = jnp.dot(
            weighted,
            values_ref[:, g * HEAD_SIZE : (g + 1) * HEAD_SIZE],
            preferred_element_type=jnp.float32,
        )
        result_ref[heads, :] = (sums + own_weight * new_values[g]) / total
    spread_blocks(result_ref[...].astype(jnp.bfloat16), row_groups, blocks_ref)


def rotation_rows(position):
    half = HEAD_SIZE // 2
    freqs = ROPE_BASE ** (-(jnp.arange(half, dtype=jnp.float32) * 2.0) / HEAD_SIZE)
    angles = position.astype(jnp.float32) * freqs
    cosine, sine = jnp.cos(angles), jnp.sin(angles)
    return jnp.stack([jnp.concatenate([cosine, cosine]), jnp.concatenate([-sine, sine])])


def body(
    hidden_in,
    norm_gain,
    w_query,
    key_weight,
    value_weight,
    w_output,
    key_cache_units,
    value_cache_units,
    key_scale,
    value_block_scale,
    lengths,
):
    row_groups, column_groups = lax.axis_size("gx"), lax.axis_size("gy")
    devices = row_groups * column_groups
    width = hidden_in.shape[1]
    slice_rows = width // row_groups // LANES
    query_cols, key_cols = w_query.shape[1], key_weight.shape[1]
    out_cols = w_output.shape[1]
    blocks_type = jax.ShapeDtypeStruct((devices, slice_rows, LANES), jnp.bfloat16)

    blocks = pl.pallas_call(
        functools.partial(norm_kernel, row_groups),
        out_shape=blocks_type,
        in_specs=[VMEM, VMEM],
        out_specs=VMEM,
        scratch_shapes=[pltpu.VMEM((width // LANES, LANES), jnp.float32)],
        compiler_params=PARAMS,
    )(hidden_in, norm_gain.reshape(-1, LANES))
    turn = rotation_rows(lengths[0])

    sent_rows = (query_cols + 2 * key_cols) // LANES
    partial = pl.pallas_call(
        project_kernel,
        out_shape=jax.ShapeDtypeStruct((devices * sent_rows, LANES), jnp.float32),
        in_specs=[VMEM] * 4,
        out_specs=VMEM,
        compiler_params=PARAMS,
    )(exchange(blocks), in_vmem(w_query), in_vmem(key_weight), in_vmem(value_weight))
    sums = exchange(partial.reshape(devices, sent_rows, 1, LANES))
    if key_cols != HEAD_SIZE:
        sums = sums.reshape(row_groups, column_groups, sent_rows * LANES)
        sums = jnp.concatenate(
            [
                part.reshape(row_groups, KEY_VALUE_HEADS, -1, HEAD_SIZE)
                for part in jnp.split(sums, (query_cols, query_cols + key_cols), axis=2)
            ],
            axis=2,
        )
    sums = sums.reshape(-1, LANES)

    attended = pl.pallas_call(
        functools.partial(attend_kernel, row_groups),
        out_shape=blocks_type,
        in_specs=[SMEM, SMEM, SMEM, VMEM, VMEM, VMEM, VMEM],
        out_specs=VMEM,
        scratch_shapes=[
            pltpu.VMEM((HQ, key_cache_units.shape[1]), jnp.float32),
            pltpu.VMEM((HQ, HEAD_SIZE), jnp.float32),
        ],
        compiler_params=PARAMS,
    )(
        lengths,
        key_scale[0].T,
        value_block_scale[0].T,
        turn,
        sums,
        in_vmem(key_cache_units[0]),
        in_vmem(value_cache_units[0]),
    )

    out_rows = out_cols // LANES
    partial = pl.pallas_call(
        output_kernel,
        out_shape=jax.ShapeDtypeStruct((devices * out_rows, LANES), jnp.float32),
        in_specs=[VMEM] * 2,
        out_specs=VMEM,
        compiler_params=PARAMS,
    )(exchange(attended), in_vmem(w_output))
    update = exchange(partial.reshape(devices, out_rows, LANES))
    update = jnp.sum(update.reshape(row_groups, column_groups * out_rows, LANES), axis=0)
    return (hidden_in.astype(jnp.float32) + update.reshape(1, width)).astype(jnp.bfloat16)


def solution(mesh):
    placed = (
        P(("gx", "gy"), None),
        P(),
        P("gx", "gy"),
        P("gx", "gy"),
        P("gx", "gy"),
        P("gx", "gy"),
        P(("gx", "gy"), None, None),
        P(("gx", "gy"), None, None),
        P(("gx", "gy"), None, None),
        P(("gx", "gy"), None, None),
        P(("gx", "gy")),
    )
    return jax.shard_map(
        body, mesh=mesh, in_specs=placed, out_specs=P(("gx", "gy"), None), check_vma=False
    )
```

```python
import functools
import math

import jax
import jax.numpy as jnp
import numpy as np
from jax import lax
from jax.experimental import pallas as pl
from jax.experimental.pallas import tpu as pltpu
from jax.sharding import PartitionSpec as P

HQ = 64
KEY_VALUE_HEADS = 8
HEAD_SIZE = 128
GROUP = HQ // KEY_VALUE_HEADS

ROPE_BASE = 500000.0
NORM_EPS = 1e-05
MASKED_SCORE = -1e30

LANES = 128
VMEM = pl.BlockSpec(memory_space=pltpu.VMEM)
ANY = pl.BlockSpec(memory_space=pl.ANY)
PARAMS = pltpu.CompilerParams(vmem_limit_bytes=4 * 1024 * 1024)
COST = pl.CostEstimate(flops=20_000_000_000, transcendentals=0, bytes_accessed=0)


def exchange(blocks):
    return lax.all_to_all(blocks, ("gx", "gy"), split_axis=0, concat_axis=0, tiled=True)


def in_vmem(array):
    return pltpu.with_memory_space_constraint(array, pltpu.VMEM)


def in_hbm(array):
    return pltpu.with_memory_space_constraint(array, pltpu.HBM)


def norm_kernel(
    row_groups,
    length_hbm,
    freqs_hbm,
    hidden_hbm,
    gain_hbm,
    blocks_ref,
    turn_ref,
    length_ref,
    freqs_ref,
    hidden_ref,
    gain_ref,
    wide_ref,
    sems,
):
    pairs = (
        (length_hbm, length_ref),
        (freqs_hbm, freqs_ref),
        (hidden_hbm, hidden_ref),
        (gain_hbm, gain_ref),
    )
    copies = [pltpu.make_async_copy(*pair, sems.at[n]) for n, pair in enumerate(pairs)]
    for copy in copies:
        copy.start()
    for copy in copies[:2]:
        copy.wait()
    length = length_ref[...].astype(jnp.float32)
    angles = length * freqs_ref[0:1, :]
    turn_ref[0:1, :] = jnp.cos(angles)
    turn_ref[1:2, :] = jnp.sin(angles) * freqs_ref[1:2, :]
    turn_ref[2:3, :] = jnp.broadcast_to(length, (1, HEAD_SIZE))
    for copy in copies[2:]:
        copy.wait()
    rows = wide_ref.shape[0]
    for row in range(rows):
        wide_ref[row : row + 1, :] = hidden_ref[:, row * LANES : (row + 1) * LANES].astype(
            jnp.float32
        )
    wide = wide_ref[...]
    variance = jnp.sum(wide * wide, keepdims=True) * (1.0 / (rows * LANES))
    normed = (wide * lax.rsqrt(variance + NORM_EPS) * gain_ref[...]).astype(jnp.bfloat16)
    spread_blocks(normed, row_groups, blocks_ref)


def spread_blocks(rows, row_groups, blocks_ref):
    per_block = rows.shape[0] // row_groups
    column_groups = blocks_ref.shape[0] // row_groups
    for i in range(row_groups):
        part = rows[i * per_block : (i + 1) * per_block]
        for j in range(column_groups):
            blocks_ref[i * column_groups + j] = part


def flat_rows(blocks_ref):
    return jnp.concatenate([blocks_ref[:, k, :] for k in range(blocks_ref.shape[1])], axis=1)


def send_rows(products, out_ref):
    requests = products[0].shape[0]
    count = out_ref.shape[0] // requests
    parts = [
        product[:, start : start + LANES]
        for product in products
        for start in range(0, product.shape[1], LANES)
    ]
    for n, part in enumerate(parts):
        out_ref[pl.ds(n, requests, stride=count), :] = part


def project_kernel(blocks_ref, w_query_ref, key_ref, value_ref, out_ref):
    rows = flat_rows(blocks_ref)
    products = [
        jnp.dot(rows, ref[...], preferred_element_type=jnp.float32)
        for ref in (w_query_ref, key_ref, value_ref)
    ]
    if products[1].shape[1] % LANES:
        products[1:] = [jnp.concatenate(products[1:], axis=1)]
    send_rows(products, out_ref)


def output_kernel(blocks_ref, weight_ref, out_ref, wide_ref):
    rows = flat_rows(blocks_ref)
    send_rows([jnp.dot(rows, weight_ref[...], preferred_element_type=jnp.float32)], wide_ref)
    out_ref[...] = wide_ref[...].astype(out_ref.dtype)


def attend_kernel(
    row_groups,
    turn_ref,
    key_scale_ref,
    value_scale_ref,
    sums_ref,
    keys_ref,
    values_ref,
    blocks_ref,
    result_ref,
    factor_ref,
):
    capacity = keys_ref.shape[0]
    scale_blocks = key_scale_ref.shape[1]
    block = capacity // scale_blocks
    inv_root = 1.0 / math.sqrt(HEAD_SIZE)
    per_group = GROUP + 2
    cosine, sine = turn_ref[0:1, :], turn_ref[1:2, :]
    length = turn_ref[2:3, 0:1].astype(jnp.int32)
    spans = [slice(b * block, (b + 1) * block) for b in range(scale_blocks)]

    def rotate(wide):
        return (wide * cosine + pltpu.roll(wide, HEAD_SIZE // 2, 1) * sine).astype(jnp.bfloat16)

    def summed(first, count):
        total = sums_ref[first : first + count, :]
        for i in range(1, row_groups):
            start = i * KEY_VALUE_HEADS * per_group + first
            total = total + sums_ref[start : start + count, :]
        return total.astype(jnp.bfloat16).astype(jnp.float32)

    shape = (KEY_VALUE_HEADS, block)
    for b, span in enumerate(spans):
        factor_ref[0:KEY_VALUE_HEADS, span] = jnp.broadcast_to(
            key_scale_ref[:, b : b + 1] * inv_root, shape
        )
        factor_ref[KEY_VALUE_HEADS:, span] = jnp.broadcast_to(value_scale_ref[:, b : b + 1], shape)

    def factors(row, span):
        return jnp.broadcast_to(factor_ref[row : row + 1, span], (GROUP, block))

    positions = lax.broadcasted_iota(jnp.int32, (GROUP, block), 1)

    def score(g):
        query = rotate(summed(g * per_group, GROUP))
        new_key = rotate(summed(g * per_group + GROUP, 1))
        own = (
            jnp.sum(
                query.astype(jnp.float32) * new_key.astype(jnp.float32), axis=1, keepdims=True
            )
            * inv_root
        )
        raw = lax.dot_general(
            query,
            keys_ref[:, g * HEAD_SIZE : (g + 1) * HEAD_SIZE],
            (((1,), (1,)), ((), ())),
            preferred_element_type=jnp.float32,
        )
        return raw, own

    def weigh(g, raw, own):
        scores = [
            jnp.where(
                positions < length - b * block, raw[:, span] * factors(g, span), MASKED_SCORE
            )
            for b, span in enumerate(spans)
        ]
        peak = jnp.maximum(
            jnp.max(functools.reduce(jnp.maximum, scores), axis=1, keepdims=True), own
        )
        probs = [jnp.exp(part - peak) for part in scores]
        own_prob = jnp.exp(own - peak)
        total = jnp.sum(functools.reduce(jnp.add, probs), axis=1, keepdims=True) + own_prob
        weighted = [
            prob * factors(KEY_VALUE_HEADS + g, span) for prob, span in zip(probs, spans)
        ]
        new_value = summed(g * per_group + GROUP + 1, 1)
        own_part = own_prob.astype(jnp.bfloat16).astype(jnp.float32) * new_value
        return weighted, own_part, total

    def finish(g, weighed):
        lhs = jnp.concatenate(
            [jnp.concatenate(parts, axis=0) for parts in zip(weighed[0][0], weighed[1][0])], axis=1
        )
        both = jnp.dot(
            lhs.astype(jnp.bfloat16),
            values_ref[:, g * HEAD_SIZE : (g + 2) * HEAD_SIZE],
            preferred_element_type=jnp.float32,
        )
        for n, (_, own_part, total) in enumerate(weighed):
            part = both[n * GROUP : (n + 1) * GROUP, n * HEAD_SIZE : (n + 1) * HEAD_SIZE]
            result_ref[(g + n) * GROUP : (g + n + 1) * GROUP, :] = (part + own_part) / total

    ahead = [score(0), score(1)]
    for g in range(0, KEY_VALUE_HEADS, 2):
        now = ahead
        if g + 2 < KEY_VALUE_HEADS:
            ahead = [score(g + 2), score(g + 3)]
        finish(g, [weigh(g + n, *now[n]) for n in range(2)])
    spread_blocks(result_ref[...].astype(jnp.bfloat16), row_groups, blocks_ref)


def rotation_rows():
    half = HEAD_SIZE // 2
    freqs = ROPE_BASE ** (-(np.arange(half) * 2.0) / HEAD_SIZE)
    signs = np.concatenate([-np.ones(half), np.ones(half)])
    return jnp.asarray(np.stack([np.tile(freqs, 2), signs]), jnp.float32)


def body(
    hidden_in,
    norm_gain,
    w_query,
    key_weight,
    value_weight,
    w_output,
    key_cache_units,
    value_cache_units,
    key_scale,
    value_block_scale,
    lengths,
):
    row_groups, column_groups = lax.axis_size("gx"), lax.axis_size("gy")
    devices = row_groups * column_groups
    width = hidden_in.shape[1]
    slice_rows = width // row_groups // LANES
    query_cols, key_cols = w_query.shape[1], key_weight.shape[1]
    out_cols = w_output.shape[1]
    blocks_type = jax.ShapeDtypeStruct((devices, slice_rows, LANES), jnp.bfloat16)

    blocks, turn = pl.pallas_call(
        functools.partial(norm_kernel, row_groups),
        out_shape=[blocks_type, jax.ShapeDtypeStruct((8, HEAD_SIZE), jnp.float32)],
        in_specs=[ANY] * 4,
        out_specs=[VMEM, VMEM],
        scratch_shapes=[
            pltpu.VMEM((1, 1), jnp.int32),
            pltpu.VMEM((2, HEAD_SIZE), jnp.float32),
            pltpu.VMEM((1, width), hidden_in.dtype),
            pltpu.VMEM((width // LANES, LANES), jnp.float32),
            pltpu.VMEM((width // LANES, LANES), jnp.float32),
            pltpu.SemaphoreType.DMA((4,)),
        ],
        compiler_params=PARAMS,
        cost_estimate=COST,
    )(
        lengths.reshape(1, 1),
        in_hbm(rotation_rows()),
        in_hbm(hidden_in),
        in_hbm(norm_gain.reshape(-1, LANES)),
    )

    sent_rows = (query_cols + 2 * key_cols) // LANES
    partial = pl.pallas_call(
        project_kernel,
        out_shape=jax.ShapeDtypeStruct((devices * sent_rows, LANES), jnp.float32),
        in_specs=[VMEM] * 4,
        out_specs=VMEM,
        compiler_params=PARAMS,
        cost_estimate=COST,
    )(exchange(blocks), in_vmem(w_query), in_vmem(key_weight), in_vmem(value_weight))
    sums = exchange(partial.reshape(devices, sent_rows, 1, LANES))
    if key_cols != HEAD_SIZE:
        sums = sums.reshape(row_groups, column_groups, sent_rows * LANES)
        sums = jnp.concatenate(
            [
                part.reshape(row_groups, KEY_VALUE_HEADS, -1, HEAD_SIZE)
                for part in jnp.split(sums, (query_cols, query_cols + key_cols), axis=2)
            ],
            axis=2,
        )
    sums = sums.reshape(-1, LANES)

    attended = pl.pallas_call(
        functools.partial(attend_kernel, row_groups),
        out_shape=blocks_type,
        in_specs=[VMEM] * 6,
        out_specs=VMEM,
        scratch_shapes=[
            pltpu.VMEM((HQ, HEAD_SIZE), jnp.float32),
            pltpu.VMEM((2 * KEY_VALUE_HEADS, key_cache_units.shape[1]), jnp.float32),
        ],
        compiler_params=PARAMS,
        cost_estimate=COST,
    )(
        turn,
        key_scale[0].T,
        value_block_scale[0].T,
        sums,
        in_vmem(key_cache_units[0]),
        in_vmem(value_cache_units[0]),
    )

    out_rows = out_cols // LANES
    partial = pl.pallas_call(
        output_kernel,
        out_shape=jax.ShapeDtypeStruct((devices * out_rows, LANES), jnp.bfloat16),
        in_specs=[VMEM] * 2,
        out_specs=VMEM,
        scratch_shapes=[pltpu.VMEM((devices * out_rows, LANES), jnp.float32)],
        compiler_params=PARAMS,
        cost_estimate=COST,
    )(exchange(attended), in_vmem(w_output))
    update = exchange(partial.reshape(devices, out_rows, LANES)).astype(jnp.float32)
    update = jnp.sum(update.reshape(row_groups, column_groups * out_rows, LANES), axis=0)
    return (hidden_in.astype(jnp.float32) + update.reshape(1, width)).astype(jnp.bfloat16)


def solution(mesh):
    placed = (
        P(("gx", "gy"), None),
        P(),
        P("gx", "gy"),
        P("gx", "gy"),
        P("gx", "gy"),
        P("gx", "gy"),
        P(("gx", "gy"), None, None),
        P(("gx", "gy"), None, None),
        P(("gx", "gy"), None, None),
        P(("gx", "gy"), None, None),
        P(("gx", "gy")),
    )
    return jax.shard_map(
        body, mesh=mesh, in_specs=placed, out_specs=P(("gx", "gy"), None), check_vma=False
    )
```

```python
import functools
import math

import jax
import jax.numpy as jnp
from jax import lax
from jax.experimental import pallas as pl
from jax.experimental.pallas import tpu as pltpu
from jax.sharding import PartitionSpec as P

HQ = 64
KEY_VALUE_HEADS = 8
HEAD_SIZE = 128
GROUP = HQ // KEY_VALUE_HEADS

ROPE_BASE = 500000.0
NORM_EPS = 1e-05
MASKED_SCORE = -1e30

LANES = 128
VMEM = pl.BlockSpec(memory_space=pltpu.VMEM)
SMEM = pl.BlockSpec(memory_space=pltpu.SMEM)
PARAMS = pltpu.CompilerParams(vmem_limit_bytes=4 * 1024 * 1024)
COST = pl.CostEstimate(flops=20_000_000_000, transcendentals=0, bytes_accessed=0)


def exchange(blocks):
    return lax.all_to_all(blocks, ("gx", "gy"), split_axis=0, concat_axis=0, tiled=True)


def in_vmem(array):
    return pltpu.with_memory_space_constraint(array, pltpu.VMEM)


def freqs_kernel(table_ref):
    half = HEAD_SIZE // 2
    lanes = lax.broadcasted_iota(jnp.int32, (1, HEAD_SIZE), 1)
    places = jnp.where(lanes < half, lanes, lanes - half)
    freqs = jnp.zeros((1, HEAD_SIZE), jnp.float32)
    for i in range(half):
        freqs = jnp.where(places == i, ROPE_BASE ** (-2.0 * i / HEAD_SIZE), freqs)
    table_ref[0:1, :] = freqs
    table_ref[1:2, :] = jnp.where(lanes < half, -1.0, 1.0)


def turn_kernel(length_ref, table_ref, turn_ref):
    length = length_ref[0].astype(jnp.float32)
    angles = length * table_ref[0:1, :]
    turn_ref[0:1, :] = jnp.cos(angles)
    turn_ref[1:2, :] = jnp.sin(angles) * table_ref[1:2, :]
    turn_ref[2:3, :] = jnp.full((1, HEAD_SIZE), length)


def norm_kernel(row_groups, turn_ref, hidden_ref, gain_ref, blocks_ref, wide_ref):
    rows = wide_ref.shape[0]
    for row in range(rows):
        wide_ref[row : row + 1, :] = hidden_ref[:, row * LANES : (row + 1) * LANES].astype(
            jnp.float32
        )
    wide = wide_ref[...]
    variance = jnp.sum(wide * wide, keepdims=True) * (1.0 / (rows * LANES))
    normed = (wide * lax.rsqrt(variance + NORM_EPS) * gain_ref[...]).astype(jnp.bfloat16)
    spread_blocks(normed, row_groups, blocks_ref)


def spread_blocks(rows, row_groups, blocks_ref):
    per_block = rows.shape[0] // row_groups
    column_groups = blocks_ref.shape[0] // row_groups
    for i in range(row_groups):
        part = rows[i * per_block : (i + 1) * per_block]
        for j in range(column_groups):
            blocks_ref[i * column_groups + j] = part


def flat_rows(blocks_ref):
    return jnp.concatenate([blocks_ref[:, k, :] for k in range(blocks_ref.shape[1])], axis=1)


def send_rows(products, out_ref):
    requests = products[0].shape[0]
    count = out_ref.shape[0] // requests
    parts = [
        product[:, start : start + LANES]
        for product in products
        for start in range(0, product.shape[1], LANES)
    ]
    for n, part in enumerate(parts):
        out_ref[pl.ds(n, requests, stride=count), :] = part


def project_kernel(blocks_ref, w_query_ref, key_ref, value_ref, out_ref):
    rows = flat_rows(blocks_ref)
    products = [
        jnp.dot(rows, ref[...], preferred_element_type=jnp.float32)
        for ref in (w_query_ref, key_ref, value_ref)
    ]
    if products[1].shape[1] % LANES:
        products[1:] = [jnp.concatenate(products[1:], axis=1)]
    send_rows(products, out_ref)


def output_kernel(blocks_ref, weight_ref, out_ref, wide_ref):
    rows = flat_rows(blocks_ref)
    send_rows([jnp.dot(rows, weight_ref[...], preferred_element_type=jnp.float32)], wide_ref)
    out_ref[...] = wide_ref[...].astype(out_ref.dtype)


def attend_kernel(
    row_groups,
    turn_ref,
    key_scale_ref,
    value_scale_ref,
    sums_ref,
    keys_ref,
    values_ref,
    blocks_ref,
    result_ref,
    factor_ref,
):
    capacity = keys_ref.shape[0]
    scale_blocks = key_scale_ref.shape[1]
    block = capacity // scale_blocks
    inv_root = 1.0 / math.sqrt(HEAD_SIZE)
    per_group = GROUP + 2
    cosine, sine = turn_ref[0:1, :], turn_ref[1:2, :]
    length = turn_ref[2:3, 0:1].astype(jnp.int32)
    spans = [slice(b * block, (b + 1) * block) for b in range(scale_blocks)]

    def rotate(wide):
        return (wide * cosine + pltpu.roll(wide, HEAD_SIZE // 2, 1) * sine).astype(jnp.bfloat16)

    def summed(first, count):
        total = sums_ref[first : first + count, :]
        for i in range(1, row_groups):
            start = i * KEY_VALUE_HEADS * per_group + first
            total = total + sums_ref[start : start + count, :]
        return total.astype(jnp.bfloat16).astype(jnp.float32)

    shape = (KEY_VALUE_HEADS, block)
    for b, span in enumerate(spans):
        factor_ref[0:KEY_VALUE_HEADS, span] = jnp.broadcast_to(
            key_scale_ref[:, b : b + 1] * inv_root, shape
        )
        factor_ref[KEY_VALUE_HEADS:, span] = jnp.broadcast_to(value_scale_ref[:, b : b + 1], shape)

    def factors(row, span):
        return jnp.broadcast_to(factor_ref[row : row + 1, span], (GROUP, block))

    positions = lax.broadcasted_iota(jnp.int32, (GROUP, block), 1)

    def score(g):
        query = rotate(summed(g * per_group, GROUP))
        new_key = rotate(summed(g * per_group + GROUP, 1))
        own = (
            jnp.sum(
                query.astype(jnp.float32) * new_key.astype(jnp.float32), axis=1, keepdims=True
            )
            * inv_root
        )
        raw = lax.dot_general(
            query,
            keys_ref[:, g * HEAD_SIZE : (g + 1) * HEAD_SIZE],
            (((1,), (1,)), ((), ())),
            preferred_element_type=jnp.float32,
        )
        return raw, own

    def weigh(g, raw, own):
        scores = [
            jnp.where(
                positions < length - b * block, raw[:, span] * factors(g, span), MASKED_SCORE
            )
            for b, span in enumerate(spans)
        ]
        peak = jnp.maximum(
            jnp.max(functools.reduce(jnp.maximum, scores), axis=1, keepdims=True), own
        )
        probs = [jnp.exp(part - peak) for part in scores]
        own_prob = jnp.exp(own - peak)
        total = jnp.sum(functools.reduce(jnp.add, probs), axis=1, keepdims=True) + own_prob
        weighted = [
            prob * factors(KEY_VALUE_HEADS + g, span) for prob, span in zip(probs, spans)
        ]
        new_value = summed(g * per_group + GROUP + 1, 1)
        own_part = own_prob.astype(jnp.bfloat16).astype(jnp.float32) * new_value
        return weighted, own_part, total

    def finish(g, weighed):
        lhs = jnp.concatenate(
            [jnp.concatenate(parts, axis=0) for parts in zip(weighed[0][0], weighed[1][0])], axis=1
        )
        both = jnp.dot(
            lhs.astype(jnp.bfloat16),
            values_ref[:, g * HEAD_SIZE : (g + 2) * HEAD_SIZE],
            preferred_element_type=jnp.float32,
        )
        for n, (_, own_part, total) in enumerate(weighed):
            part = both[n * GROUP : (n + 1) * GROUP, n * HEAD_SIZE : (n + 1) * HEAD_SIZE]
            result_ref[(g + n) * GROUP : (g + n + 1) * GROUP, :] = (part + own_part) / total

    ahead = [score(0), score(1)]
    for g in range(0, KEY_VALUE_HEADS, 2):
        now = ahead
        if g + 2 < KEY_VALUE_HEADS:
            ahead = [score(g + 2), score(g + 3)]
        finish(g, [weigh(g + n, *now[n]) for n in range(2)])
    spread_blocks(result_ref[...].astype(jnp.bfloat16), row_groups, blocks_ref)


def body(
    hidden_in,
    norm_gain,
    w_query,
    key_weight,
    value_weight,
    w_output,
    key_cache_units,
    value_cache_units,
    key_scale,
    value_block_scale,
    lengths,
):
    row_groups, column_groups = lax.axis_size("gx"), lax.axis_size("gy")
    devices = row_groups * column_groups
    width = hidden_in.shape[1]
    slice_rows = width // row_groups // LANES
    query_cols, key_cols = w_query.shape[1], key_weight.shape[1]
    out_cols = w_output.shape[1]
    blocks_type = jax.ShapeDtypeStruct((devices, slice_rows, LANES), jnp.bfloat16)

    turn_type = jax.ShapeDtypeStruct((8, HEAD_SIZE), jnp.float32)
    table = pl.pallas_call(
        freqs_kernel,
        out_shape=turn_type,
        out_specs=VMEM,
        compiler_params=PARAMS,
        cost_estimate=COST,
    )()
    lengths, table = lax.optimization_barrier((lengths, table))
    turn = pl.pallas_call(
        turn_kernel,
        out_shape=turn_type,
        in_specs=[SMEM, VMEM],
        out_specs=VMEM,
        compiler_params=PARAMS,
    )(lengths, table)
    blocks = pl.pallas_call(
        functools.partial(norm_kernel, row_groups),
        out_shape=blocks_type,
        in_specs=[VMEM] * 3,
        out_specs=VMEM,
        scratch_shapes=[pltpu.VMEM((width // LANES, LANES), jnp.float32)],
        compiler_params=PARAMS,
        cost_estimate=COST,
    )(turn, in_vmem(hidden_in), in_vmem(norm_gain.reshape(-1, LANES)))

    sent_rows = (query_cols + 2 * key_cols) // LANES
    partial = pl.pallas_call(
        project_kernel,
        out_shape=jax.ShapeDtypeStruct((devices * sent_rows, LANES), jnp.float32),
        in_specs=[VMEM] * 4,
        out_specs=VMEM,
        compiler_params=PARAMS,
        cost_estimate=COST,
    )(exchange(blocks), in_vmem(w_query), in_vmem(key_weight), in_vmem(value_weight))
    sums = exchange(partial.reshape(devices, sent_rows, 1, LANES))
    if key_cols != HEAD_SIZE:
        sums = sums.reshape(row_groups, column_groups, sent_rows * LANES)
        sums = jnp.concatenate(
            [
                part.reshape(row_groups, KEY_VALUE_HEADS, -1, HEAD_SIZE)
                for part in jnp.split(sums, (query_cols, query_cols + key_cols), axis=2)
            ],
            axis=2,
        )
    sums = sums.reshape(-1, LANES)

    attended = pl.pallas_call(
        functools.partial(attend_kernel, row_groups),
        out_shape=blocks_type,
        in_specs=[VMEM] * 6,
        out_specs=VMEM,
        scratch_shapes=[
            pltpu.VMEM((HQ, HEAD_SIZE), jnp.float32),
            pltpu.VMEM((2 * KEY_VALUE_HEADS, key_cache_units.shape[1]), jnp.float32),
        ],
        compiler_params=PARAMS,
        cost_estimate=COST,
    )(
        turn,
        key_scale[0].T,
        value_block_scale[0].T,
        sums,
        in_vmem(key_cache_units[0]),
        in_vmem(value_cache_units[0]),
    )

    out_rows = out_cols // LANES
    partial = pl.pallas_call(
        output_kernel,
        out_shape=jax.ShapeDtypeStruct((devices * out_rows, LANES), jnp.bfloat16),
        in_specs=[VMEM] * 2,
        out_specs=VMEM,
        scratch_shapes=[pltpu.VMEM((devices * out_rows, LANES), jnp.float32)],
        compiler_params=PARAMS,
        cost_estimate=COST,
    )(exchange(attended), in_vmem(w_output))
    update = exchange(partial.reshape(devices, out_rows, LANES)).astype(jnp.float32)
    update = jnp.sum(update.reshape(row_groups, column_groups * out_rows, LANES), axis=0)
    return (hidden_in.astype(jnp.float32) + update.reshape(1, width)).astype(jnp.bfloat16)


def solution(mesh):
    placed = (
        P(("gx", "gy"), None),
        P(),
        P("gx", "gy"),
        P("gx", "gy"),
        P("gx", "gy"),
        P("gx", "gy"),
        P(("gx", "gy"), None, None),
        P(("gx", "gy"), None, None),
        P(("gx", "gy"), None, None),
        P(("gx", "gy"), None, None),
        P(("gx", "gy")),
    )
    return jax.shard_map(
        body, mesh=mesh, in_specs=placed, out_specs=P(("gx", "gy"), None), check_vma=False
    )
```

```python
import functools
import math

import jax
import jax.numpy as jnp
from jax import lax
from jax.experimental import pallas as pl
from jax.experimental.pallas import tpu as pltpu
from jax.sharding import PartitionSpec as P

HQ = 64
KEY_VALUE_HEADS = 8
HEAD_SIZE = 128
GROUP = HQ // KEY_VALUE_HEADS

ROPE_BASE = 500000.0
NORM_EPS = 1e-05
MASKED_SCORE = -1e30

LANES = 128
VMEM = pl.BlockSpec(memory_space=pltpu.VMEM)
SMEM = pl.BlockSpec(memory_space=pltpu.SMEM)
PARAMS = pltpu.CompilerParams(vmem_limit_bytes=4 * 1024 * 1024)
SENT_SCALE = 16.0
COST = pl.CostEstimate(flops=20_000_000_000, transcendentals=0, bytes_accessed=0)


def exchange(blocks):
    return lax.all_to_all(blocks, ("gx", "gy"), split_axis=0, concat_axis=0, tiled=True)


def exchange_sums(partial, devices):
    sent = (partial * SENT_SCALE).astype(jnp.float16)
    count = partial.shape[0] // devices
    pair = 8 if count % 8 == 0 else 2 if count % 2 == 0 else 1
    arrived = exchange(sent.reshape(devices, -1, pair, LANES)).reshape(partial.shape)
    return arrived.astype(jnp.float32) * (1.0 / SENT_SCALE)


def in_vmem(array):
    return pltpu.with_memory_space_constraint(array, pltpu.VMEM)


def freqs_kernel(table_ref):
    half = HEAD_SIZE // 2
    lanes = lax.broadcasted_iota(jnp.int32, (1, HEAD_SIZE), 1)
    places = jnp.where(lanes < half, lanes, lanes - half)
    freqs = jnp.zeros((1, HEAD_SIZE), jnp.float32)
    for i in range(half):
        freqs = jnp.where(places == i, ROPE_BASE ** (-2.0 * i / HEAD_SIZE), freqs)
    table_ref[0:1, :] = freqs
    table_ref[1:2, :] = jnp.where(lanes < half, -1.0, 1.0)


def turn_kernel(length_ref, table_ref, turn_ref):
    length = length_ref[0].astype(jnp.float32)
    angles = length * table_ref[0:1, :]
    turn_ref[0:1, :] = jnp.cos(angles)
    turn_ref[1:2, :] = jnp.sin(angles) * table_ref[1:2, :]
    turn_ref[2:3, :] = jnp.full((1, HEAD_SIZE), length)


def norm_kernel(row_groups, turn_ref, hidden_ref, gain_ref, blocks_ref, wide_ref):
    rows = wide_ref.shape[0]
    for row in range(rows):
        wide_ref[row : row + 1, :] = hidden_ref[:, row * LANES : (row + 1) * LANES].astype(
            jnp.float32
        )
    wide = wide_ref[...]
    variance = jnp.sum(wide * wide, keepdims=True) * (1.0 / (rows * LANES))
    normed = (wide * lax.rsqrt(variance + NORM_EPS) * gain_ref[...]).astype(jnp.bfloat16)
    spread_blocks(normed, row_groups, blocks_ref)


def spread_blocks(rows, row_groups, blocks_ref):
    per_block = rows.shape[0] // row_groups
    column_groups = blocks_ref.shape[0] // row_groups
    for i in range(row_groups):
        part = rows[i * per_block : (i + 1) * per_block]
        for j in range(column_groups):
            blocks_ref[i * column_groups + j] = part


def flat_rows(blocks_ref):
    return jnp.concatenate([blocks_ref[:, k, :] for k in range(blocks_ref.shape[1])], axis=1)


def send_rows(products, out_ref):
    requests = products[0].shape[0]
    count = out_ref.shape[0] // requests
    parts = [
        product[:, start : start + LANES]
        for product in products
        for start in range(0, product.shape[1], LANES)
    ]
    for n, part in enumerate(parts):
        out_ref[pl.ds(n, requests, stride=count), :] = part


def project_kernel(blocks_ref, w_query_ref, key_ref, value_ref, out_ref):
    rows = flat_rows(blocks_ref)
    products = [
        jnp.dot(rows, ref[...], preferred_element_type=jnp.float32)
        for ref in (w_query_ref, key_ref, value_ref)
    ]
    if products[1].shape[1] % LANES:
        products[1:] = [jnp.concatenate(products[1:], axis=1)]
    send_rows(products, out_ref)


def output_kernel(blocks_ref, weight_ref, out_ref):
    rows = flat_rows(blocks_ref)
    send_rows([jnp.dot(rows, weight_ref[...], preferred_element_type=jnp.float32)], out_ref)


def attend_kernel(
    row_groups,
    turn_ref,
    key_scale_ref,
    value_scale_ref,
    sums_ref,
    keys_ref,
    values_ref,
    blocks_ref,
    result_ref,
    factor_ref,
):
    capacity = keys_ref.shape[0]
    scale_blocks = key_scale_ref.shape[1]
    block = capacity // scale_blocks
    inv_root = 1.0 / math.sqrt(HEAD_SIZE)
    per_group = GROUP + 2
    cosine, sine = turn_ref[0:1, :], turn_ref[1:2, :]
    length = turn_ref[2:3, 0:1].astype(jnp.int32)
    spans = [slice(b * block, (b + 1) * block) for b in range(scale_blocks)]

    def rotate(wide):
        return (wide * cosine + pltpu.roll(wide, HEAD_SIZE // 2, 1) * sine).astype(jnp.bfloat16)

    def summed(first, count):
        total = sums_ref[first : first + count, :]
        for i in range(1, row_groups):
            start = i * KEY_VALUE_HEADS * per_group + first
            total = total + sums_ref[start : start + count, :]
        return total.astype(jnp.bfloat16).astype(jnp.float32)

    shape = (KEY_VALUE_HEADS, block)
    for b, span in enumerate(spans):
        factor_ref[0:KEY_VALUE_HEADS, span] = jnp.broadcast_to(
            key_scale_ref[:, b : b + 1] * inv_root, shape
        )
        factor_ref[KEY_VALUE_HEADS:, span] = jnp.broadcast_to(value_scale_ref[:, b : b + 1], shape)

    def factors(row, span):
        return jnp.broadcast_to(factor_ref[row : row + 1, span], (GROUP, block))

    positions = lax.broadcasted_iota(jnp.int32, (GROUP, block), 1)

    def score(g):
        query = rotate(summed(g * per_group, GROUP))
        new_key = rotate(summed(g * per_group + GROUP, 1))
        own = (
            jnp.sum(
                query.astype(jnp.float32) * new_key.astype(jnp.float32), axis=1, keepdims=True
            )
            * inv_root
        )
        raw = lax.dot_general(
            query,
            keys_ref[:, g * HEAD_SIZE : (g + 1) * HEAD_SIZE],
            (((1,), (1,)), ((), ())),
            preferred_element_type=jnp.float32,
        )
        return raw, own

    def weigh(g, raw, own):
        scores = [
            jnp.where(
                positions < length - b * block, raw[:, span] * factors(g, span), MASKED_SCORE
            )
            for b, span in enumerate(spans)
        ]
        peak = jnp.maximum(
            jnp.max(functools.reduce(jnp.maximum, scores), axis=1, keepdims=True), own
        )
        probs = [jnp.exp(part - peak) for part in scores]
        own_prob = jnp.exp(own - peak)
        total = jnp.sum(functools.reduce(jnp.add, probs), axis=1, keepdims=True) + own_prob
        weighted = [
            prob * factors(KEY_VALUE_HEADS + g, span) for prob, span in zip(probs, spans)
        ]
        new_value = summed(g * per_group + GROUP + 1, 1)
        own_part = own_prob.astype(jnp.bfloat16).astype(jnp.float32) * new_value
        return weighted, own_part, total

    def finish(g, weighed):
        lhs = jnp.concatenate(
            [jnp.concatenate(parts, axis=0) for parts in zip(weighed[0][0], weighed[1][0])], axis=1
        )
        both = jnp.dot(
            lhs.astype(jnp.bfloat16),
            values_ref[:, g * HEAD_SIZE : (g + 2) * HEAD_SIZE],
            preferred_element_type=jnp.float32,
        )
        for n, (_, own_part, total) in enumerate(weighed):
            part = both[n * GROUP : (n + 1) * GROUP, n * HEAD_SIZE : (n + 1) * HEAD_SIZE]
            result_ref[(g + n) * GROUP : (g + n + 1) * GROUP, :] = (part + own_part) / total

    ahead = [score(0), score(1)]
    for g in range(0, KEY_VALUE_HEADS, 2):
        now = ahead
        if g + 2 < KEY_VALUE_HEADS:
            ahead = [score(g + 2), score(g + 3)]
        finish(g, [weigh(g + n, *now[n]) for n in range(2)])
    spread_blocks(result_ref[...].astype(jnp.bfloat16), row_groups, blocks_ref)


def body(
    hidden_in,
    norm_gain,
    w_query,
    key_weight,
    value_weight,
    w_output,
    key_cache_units,
    value_cache_units,
    key_scale,
    value_block_scale,
    lengths,
):
    row_groups, column_groups = lax.axis_size("gx"), lax.axis_size("gy")
    devices = row_groups * column_groups
    width = hidden_in.shape[1]
    slice_rows = width // row_groups // LANES
    query_cols, key_cols = w_query.shape[1], key_weight.shape[1]
    out_cols = w_output.shape[1]
    blocks_type = jax.ShapeDtypeStruct((devices, slice_rows, LANES), jnp.bfloat16)

    turn_type = jax.ShapeDtypeStruct((8, HEAD_SIZE), jnp.float32)
    table = pl.pallas_call(
        freqs_kernel,
        out_shape=turn_type,
        out_specs=VMEM,
        compiler_params=PARAMS,
        cost_estimate=COST,
    )()
    lengths, table = lax.optimization_barrier((lengths, table))
    turn = pl.pallas_call(
        turn_kernel,
        out_shape=turn_type,
        in_specs=[SMEM, VMEM],
        out_specs=VMEM,
        compiler_params=PARAMS,
    )(lengths, table)
    blocks = pl.pallas_call(
        functools.partial(norm_kernel, row_groups),
        out_shape=blocks_type,
        in_specs=[VMEM] * 3,
        out_specs=VMEM,
        scratch_shapes=[pltpu.VMEM((width // LANES, LANES), jnp.float32)],
        compiler_params=PARAMS,
        cost_estimate=COST,
    )(turn, in_vmem(hidden_in), in_vmem(norm_gain.reshape(-1, LANES)))

    sent_rows = (query_cols + 2 * key_cols) // LANES
    partial = pl.pallas_call(
        project_kernel,
        out_shape=jax.ShapeDtypeStruct((devices * sent_rows, LANES), jnp.float32),
        in_specs=[VMEM] * 4,
        out_specs=VMEM,
        compiler_params=PARAMS,
        cost_estimate=COST,
    )(exchange(blocks), in_vmem(w_query), in_vmem(key_weight), in_vmem(value_weight))
    sums = exchange_sums(partial, devices)
    if key_cols != HEAD_SIZE:
        sums = sums.reshape(row_groups, column_groups, sent_rows * LANES)
        sums = jnp.concatenate(
            [
                part.reshape(row_groups, KEY_VALUE_HEADS, -1, HEAD_SIZE)
                for part in jnp.split(sums, (query_cols, query_cols + key_cols), axis=2)
            ],
            axis=2,
        )
    sums = sums.reshape(-1, LANES)

    attended = pl.pallas_call(
        functools.partial(attend_kernel, row_groups),
        out_shape=blocks_type,
        in_specs=[VMEM] * 6,
        out_specs=VMEM,
        scratch_shapes=[
            pltpu.VMEM((HQ, HEAD_SIZE), jnp.float32),
            pltpu.VMEM((2 * KEY_VALUE_HEADS, key_cache_units.shape[1]), jnp.float32),
        ],
        compiler_params=PARAMS,
        cost_estimate=COST,
    )(
        turn,
        key_scale[0].T,
        value_block_scale[0].T,
        sums,
        in_vmem(key_cache_units[0]),
        in_vmem(value_cache_units[0]),
    )

    out_rows = out_cols // LANES
    partial = pl.pallas_call(
        output_kernel,
        out_shape=jax.ShapeDtypeStruct((devices * out_rows, LANES), jnp.float32),
        in_specs=[VMEM] * 2,
        out_specs=VMEM,
        compiler_params=PARAMS,
        cost_estimate=COST,
    )(exchange(attended), in_vmem(w_output))
    update = exchange_sums(partial, devices)
    update = jnp.sum(update.reshape(row_groups, column_groups * out_rows, LANES), axis=0)
    return (hidden_in.astype(jnp.float32) + update.reshape(1, width)).astype(jnp.bfloat16)


def solution(mesh):
    placed = (
        P(("gx", "gy"), None),
        P(),
        P("gx", "gy"),
        P("gx", "gy"),
        P("gx", "gy"),
        P("gx", "gy"),
        P(("gx", "gy"), None, None),
        P(("gx", "gy"), None, None),
        P(("gx", "gy"), None, None),
        P(("gx", "gy"), None, None),
        P(("gx", "gy")),
    )
    return jax.shard_map(
        body, mesh=mesh, in_specs=placed, out_specs=P(("gx", "gy"), None), check_vma=False
    )
```

```python
import functools
import math

import jax
import jax.numpy as jnp
from jax import lax
from jax.experimental import pallas as pl
from jax.experimental.pallas import tpu as pltpu
from jax.sharding import PartitionSpec as P

HQ = 64
KEY_VALUE_HEADS = 8
HEAD_SIZE = 128
GROUP = HQ // KEY_VALUE_HEADS

ROPE_BASE = 500000.0
NORM_EPS = 1e-05
MASKED_SCORE = -1e30

LANES = 128
VMEM = pl.BlockSpec(memory_space=pltpu.VMEM)
SMEM = pl.BlockSpec(memory_space=pltpu.SMEM)
PARAMS = pltpu.CompilerParams(vmem_limit_bytes=4 * 1024 * 1024)
SENT_SCALE = 16.0
COST = pl.CostEstimate(flops=20_000_000_000, transcendentals=0, bytes_accessed=0)


def exchange(blocks):
    return lax.all_to_all(blocks, ("gx", "gy"), split_axis=0, concat_axis=0, tiled=True)


def exchange_sums(partial, devices):
    sent = (partial * SENT_SCALE).astype(jnp.float16)
    count = partial.shape[0] // devices
    pair = 8 if count % 8 == 0 else 2 if count % 2 == 0 else 1
    arrived = exchange(sent.reshape(devices, -1, pair, LANES)).reshape(partial.shape)
    return arrived.astype(jnp.float32) * (1.0 / SENT_SCALE)


def in_vmem(array):
    return pltpu.with_memory_space_constraint(array, pltpu.VMEM)


def freqs_kernel(table_ref):
    half = HEAD_SIZE // 2
    lanes = lax.broadcasted_iota(jnp.int32, (1, HEAD_SIZE), 1)
    places = jnp.where(lanes < half, lanes, lanes - half)
    freqs = jnp.zeros((1, HEAD_SIZE), jnp.float32)
    for i in range(half):
        freqs = jnp.where(places == i, ROPE_BASE ** (-2.0 * i / HEAD_SIZE), freqs)
    table_ref[0:1, :] = freqs
    table_ref[1:2, :] = jnp.where(lanes < half, -1.0, 1.0)


def turn_kernel(length_ref, table_ref, turn_ref):
    length = length_ref[0].astype(jnp.float32)
    angles = length * table_ref[0:1, :]
    turn_ref[0:1, :] = jnp.cos(angles)
    turn_ref[1:2, :] = jnp.sin(angles) * table_ref[1:2, :]
    turn_ref[2:3, :] = jnp.full((1, HEAD_SIZE), length)


def norm_kernel(row_groups, turn_ref, hidden_ref, gain_ref, blocks_ref, wide_ref):
    rows = wide_ref.shape[0]
    for row in range(rows):
        wide_ref[row : row + 1, :] = hidden_ref[:, row * LANES : (row + 1) * LANES].astype(
            jnp.float32
        )
    wide = wide_ref[...]
    variance = jnp.sum(wide * wide, keepdims=True) * (1.0 / (rows * LANES))
    normed = (wide * lax.rsqrt(variance + NORM_EPS) * gain_ref[...]).astype(jnp.bfloat16)
    spread_blocks(normed, row_groups, blocks_ref)


def spread_blocks(rows, row_groups, blocks_ref):
    per_block = rows.shape[0] // row_groups
    column_groups = blocks_ref.shape[0] // row_groups
    for i in range(row_groups):
        part = rows[i * per_block : (i + 1) * per_block]
        for j in range(column_groups):
            blocks_ref[i * column_groups + j] = part


def flat_rows(blocks_ref):
    return jnp.concatenate([blocks_ref[:, k, :] for k in range(blocks_ref.shape[1])], axis=1)


def spaced(requests, count):
    return pltpu.VMEM(((requests + 1) * count, LANES), jnp.float32)


def send_rows(products, out_ref, spaced_ref):
    requests = products[0].shape[0]
    count = out_ref.shape[0] // requests
    parts = [
        product[:, start : start + LANES]
        for product in products
        for start in range(0, product.shape[1], LANES)
    ]
    for n, part in enumerate(parts):
        spaced_ref[pl.ds(n, requests, stride=count), :] = part
    out_ref[...] = spaced_ref[: requests * count, :]


def project_kernel(blocks_ref, w_query_ref, key_ref, value_ref, out_ref, spaced_ref):
    rows = flat_rows(blocks_ref)
    products = [
        jnp.dot(rows, ref[...], preferred_element_type=jnp.float32)
        for ref in (w_query_ref, key_ref, value_ref)
    ]
    if products[1].shape[1] % LANES:
        products[1:] = [jnp.concatenate(products[1:], axis=1)]
    send_rows(products, out_ref, spaced_ref)


def output_kernel(blocks_ref, weight_ref, out_ref, spaced_ref):
    rows = flat_rows(blocks_ref)
    product = jnp.dot(rows, weight_ref[...], preferred_element_type=jnp.float32)
    send_rows([product], out_ref, spaced_ref)


def attend_kernel(
    row_groups,
    turn_ref,
    key_scale_ref,
    value_scale_ref,
    sums_ref,
    keys_ref,
    values_ref,
    blocks_ref,
    result_ref,
    factor_ref,
):
    capacity = keys_ref.shape[0]
    scale_blocks = key_scale_ref.shape[1]
    block = capacity // scale_blocks
    inv_root = 1.0 / math.sqrt(HEAD_SIZE)
    per_group = GROUP + 2
    cosine, sine = turn_ref[0:1, :], turn_ref[1:2, :]
    length = turn_ref[2:3, 0:1].astype(jnp.int32)
    spans = [slice(b * block, (b + 1) * block) for b in range(scale_blocks)]

    def rotate(wide):
        return (wide * cosine + pltpu.roll(wide, HEAD_SIZE // 2, 1) * sine).astype(jnp.bfloat16)

    def summed(first, count):
        total = sums_ref[first : first + count, :]
        for i in range(1, row_groups):
            start = i * KEY_VALUE_HEADS * per_group + first
            total = total + sums_ref[start : start + count, :]
        return total.astype(jnp.bfloat16).astype(jnp.float32)

    shape = (KEY_VALUE_HEADS, block)
    for b, span in enumerate(spans):
        factor_ref[0:KEY_VALUE_HEADS, span] = jnp.broadcast_to(
            key_scale_ref[:, b : b + 1] * inv_root, shape
        )
        factor_ref[KEY_VALUE_HEADS:, span] = jnp.broadcast_to(value_scale_ref[:, b : b + 1], shape)

    def factors(row, span):
        return jnp.broadcast_to(factor_ref[row : row + 1, span], (GROUP, block))

    positions = lax.broadcasted_iota(jnp.int32, (GROUP, block), 1)

    def score(g):
        query = rotate(summed(g * per_group, GROUP))
        new_key = rotate(summed(g * per_group + GROUP, 1))
        own = (
            jnp.sum(
                query.astype(jnp.float32) * new_key.astype(jnp.float32), axis=1, keepdims=True
            )
            * inv_root
        )
        raw = lax.dot_general(
            query,
            keys_ref[:, g * HEAD_SIZE : (g + 1) * HEAD_SIZE],
            (((1,), (1,)), ((), ())),
            preferred_element_type=jnp.float32,
        )
        return raw, own

    def weigh(g, raw, own):
        scores = [
            jnp.where(
                positions < length - b * block, raw[:, span] * factors(g, span), MASKED_SCORE
            )
            for b, span in enumerate(spans)
        ]
        peak = jnp.maximum(
            jnp.max(functools.reduce(jnp.maximum, scores), axis=1, keepdims=True), own
        )
        probs = [jnp.exp(part - peak) for part in scores]
        own_prob = jnp.exp(own - peak)
        total = jnp.sum(functools.reduce(jnp.add, probs), axis=1, keepdims=True) + own_prob
        weighted = [
            prob * factors(KEY_VALUE_HEADS + g, span) for prob, span in zip(probs, spans)
        ]
        new_value = summed(g * per_group + GROUP + 1, 1)
        own_part = own_prob.astype(jnp.bfloat16).astype(jnp.float32) * new_value
        return weighted, own_part, total

    def finish(g, weighed):
        lhs = jnp.concatenate(
            [jnp.concatenate(parts, axis=0) for parts in zip(weighed[0][0], weighed[1][0])], axis=1
        )
        both = jnp.dot(
            lhs.astype(jnp.bfloat16),
            values_ref[:, g * HEAD_SIZE : (g + 2) * HEAD_SIZE],
            preferred_element_type=jnp.float32,
        )
        for n, (_, own_part, total) in enumerate(weighed):
            part = both[n * GROUP : (n + 1) * GROUP, n * HEAD_SIZE : (n + 1) * HEAD_SIZE]
            result_ref[(g + n) * GROUP : (g + n + 1) * GROUP, :] = (part + own_part) / total

    ahead = [score(0), score(1)]
    for g in range(0, KEY_VALUE_HEADS, 2):
        now = ahead
        if g + 2 < KEY_VALUE_HEADS:
            ahead = [score(g + 2), score(g + 3)]
        finish(g, [weigh(g + n, *now[n]) for n in range(2)])
    spread_blocks(result_ref[...].astype(jnp.bfloat16), row_groups, blocks_ref)


def body(
    hidden_in,
    norm_gain,
    w_query,
    key_weight,
    value_weight,
    w_output,
    key_cache_units,
    value_cache_units,
    key_scale,
    value_block_scale,
    lengths,
):
    row_groups, column_groups = lax.axis_size("gx"), lax.axis_size("gy")
    devices = row_groups * column_groups
    width = hidden_in.shape[1]
    slice_rows = width // row_groups // LANES
    query_cols, key_cols = w_query.shape[1], key_weight.shape[1]
    out_cols = w_output.shape[1]
    blocks_type = jax.ShapeDtypeStruct((devices, slice_rows, LANES), jnp.bfloat16)

    turn_type = jax.ShapeDtypeStruct((8, HEAD_SIZE), jnp.float32)
    table = pl.pallas_call(
        freqs_kernel,
        out_shape=turn_type,
        out_specs=VMEM,
        compiler_params=PARAMS,
        cost_estimate=COST,
    )()
    lengths, table = lax.optimization_barrier((lengths, table))
    turn = pl.pallas_call(
        turn_kernel,
        out_shape=turn_type,
        in_specs=[SMEM, VMEM],
        out_specs=VMEM,
        compiler_params=PARAMS,
    )(lengths, table)
    blocks = pl.pallas_call(
        functools.partial(norm_kernel, row_groups),
        out_shape=blocks_type,
        in_specs=[VMEM] * 3,
        out_specs=VMEM,
        scratch_shapes=[pltpu.VMEM((width // LANES, LANES), jnp.float32)],
        compiler_params=PARAMS,
        cost_estimate=COST,
    )(turn, in_vmem(hidden_in), in_vmem(norm_gain.reshape(-1, LANES)))

    sent_rows = (query_cols + 2 * key_cols) // LANES
    partial = pl.pallas_call(
        project_kernel,
        out_shape=jax.ShapeDtypeStruct((devices * sent_rows, LANES), jnp.float32),
        in_specs=[VMEM] * 4,
        out_specs=VMEM,
        scratch_shapes=[spaced(devices, sent_rows)],
        compiler_params=PARAMS,
        cost_estimate=COST,
    )(exchange(blocks), in_vmem(w_query), in_vmem(key_weight), in_vmem(value_weight))
    sums = exchange_sums(partial, devices)
    if key_cols != HEAD_SIZE:
        sums = sums.reshape(row_groups, column_groups, sent_rows * LANES)
        sums = jnp.concatenate(
            [
                part.reshape(row_groups, KEY_VALUE_HEADS, -1, HEAD_SIZE)
                for part in jnp.split(sums, (query_cols, query_cols + key_cols), axis=2)
            ],
            axis=2,
        )
    sums = sums.reshape(-1, LANES)

    attended = pl.pallas_call(
        functools.partial(attend_kernel, row_groups),
        out_shape=blocks_type,
        in_specs=[VMEM] * 6,
        out_specs=VMEM,
        scratch_shapes=[
            pltpu.VMEM((HQ, HEAD_SIZE), jnp.float32),
            pltpu.VMEM((2 * KEY_VALUE_HEADS, key_cache_units.shape[1]), jnp.float32),
        ],
        compiler_params=PARAMS,
        cost_estimate=COST,
    )(
        turn,
        key_scale[0].T,
        value_block_scale[0].T,
        sums,
        in_vmem(key_cache_units[0]),
        in_vmem(value_cache_units[0]),
    )

    out_rows = out_cols // LANES
    partial = pl.pallas_call(
        output_kernel,
        out_shape=jax.ShapeDtypeStruct((devices * out_rows, LANES), jnp.float32),
        in_specs=[VMEM] * 2,
        out_specs=VMEM,
        scratch_shapes=[spaced(devices, out_rows)],
        compiler_params=PARAMS,
        cost_estimate=COST,
    )(exchange(attended), in_vmem(w_output))
    update = exchange_sums(partial, devices)
    update = jnp.sum(update.reshape(row_groups, column_groups * out_rows, LANES), axis=0)
    return (hidden_in.astype(jnp.float32) + update.reshape(1, width)).astype(jnp.bfloat16)


def solution(mesh):
    placed = (
        P(("gx", "gy"), None),
        P(),
        P("gx", "gy"),
        P("gx", "gy"),
        P("gx", "gy"),
        P("gx", "gy"),
        P(("gx", "gy"), None, None),
        P(("gx", "gy"), None, None),
        P(("gx", "gy"), None, None),
        P(("gx", "gy"), None, None),
        P(("gx", "gy")),
    )
    return jax.shard_map(
        body, mesh=mesh, in_specs=placed, out_specs=P(("gx", "gy"), None), check_vma=False
    )
```

```python
import functools
import math

import jax
import jax.numpy as jnp
from jax import lax
from jax.experimental import pallas as pl
from jax.experimental.pallas import tpu as pltpu
from jax.sharding import PartitionSpec as P

HQ = 64
KEY_VALUE_HEADS = 8
HEAD_SIZE = 128
GROUP = HQ // KEY_VALUE_HEADS

ROPE_BASE = 500000.0
NORM_EPS = 1e-05
MASKED_SCORE = -1e30

LANES = 128
VMEM = pl.BlockSpec(memory_space=pltpu.VMEM)
SMEM = pl.BlockSpec(memory_space=pltpu.SMEM)
PARAMS = pltpu.CompilerParams(vmem_limit_bytes=4 * 1024 * 1024)
COST = pl.CostEstimate(flops=20_000_000_000, transcendentals=0, bytes_accessed=0)


def exchange(blocks):
    return lax.all_to_all(blocks, ("gx", "gy"), split_axis=0, concat_axis=0, tiled=True)


def in_vmem(array):
    return pltpu.with_memory_space_constraint(array, pltpu.VMEM)


def freqs_kernel(table_ref):
    half = HEAD_SIZE // 2
    lanes = lax.broadcasted_iota(jnp.int32, (1, HEAD_SIZE), 1)
    places = jnp.where(lanes < half, lanes, lanes - half)
    freqs = jnp.zeros((1, HEAD_SIZE), jnp.float32)
    for i in range(half):
        freqs = jnp.where(places == i, ROPE_BASE ** (-2.0 * i / HEAD_SIZE), freqs)
    table_ref[0:1, :] = freqs
    table_ref[1:2, :] = jnp.where(lanes < half, -1.0, 1.0)


def turn_kernel(length_ref, table_ref, turn_ref):
    length = length_ref[0].astype(jnp.float32)
    angles = length * table_ref[0:1, :]
    turn_ref[0:1, :] = jnp.cos(angles)
    turn_ref[1:2, :] = jnp.sin(angles) * table_ref[1:2, :]
    turn_ref[2:3, :] = jnp.full((1, HEAD_SIZE), length)


def norm_kernel(row_groups, turn_ref, hidden_ref, gain_ref, blocks_ref, wide_ref):
    rows = wide_ref.shape[0]
    for row in range(rows):
        wide_ref[row : row + 1, :] = hidden_ref[:, row * LANES : (row + 1) * LANES].astype(
            jnp.float32
        )
    wide = wide_ref[...]
    variance = jnp.sum(wide * wide, keepdims=True) * (1.0 / (rows * LANES))
    normed = (wide * lax.rsqrt(variance + NORM_EPS) * gain_ref[...]).astype(jnp.bfloat16)
    spread_blocks(normed, row_groups, blocks_ref)


def spread_blocks(rows, row_groups, blocks_ref):
    per_block = rows.shape[0] // row_groups
    column_groups = blocks_ref.shape[0] // row_groups
    for i in range(row_groups):
        part = rows[i * per_block : (i + 1) * per_block]
        for j in range(column_groups):
            blocks_ref[i * column_groups + j] = part


def flat_rows(blocks_ref):
    return jnp.concatenate([blocks_ref[:, k, :] for k in range(blocks_ref.shape[1])], axis=1)


def spaced(requests, count):
    return pltpu.VMEM(((requests + 1) * count, LANES), jnp.float32)


def send_rows(products, out_ref, spaced_ref):
    requests = products[0].shape[0]
    count = out_ref.shape[0] // requests
    parts = [
        product[:, start : start + LANES]
        for product in products
        for start in range(0, product.shape[1], LANES)
    ]
    for n, part in enumerate(parts):
        spaced_ref[pl.ds(n, requests, stride=count), :] = part
    out_ref[...] = spaced_ref[: requests * count, :].astype(out_ref.dtype)


def project_kernel(blocks_ref, w_query_ref, key_ref, value_ref, out_ref, spaced_ref):
    rows = flat_rows(blocks_ref)
    products = [
        jnp.dot(rows, ref[...], preferred_element_type=jnp.float32)
        for ref in (w_query_ref, key_ref, value_ref)
    ]
    if products[1].shape[1] % LANES:
        products[1:] = [jnp.concatenate(products[1:], axis=1)]
    send_rows(products, out_ref, spaced_ref)


def output_kernel(blocks_ref, weight_ref, out_ref, spaced_ref):
    rows = flat_rows(blocks_ref)
    product = jnp.dot(rows, weight_ref[...], preferred_element_type=jnp.float32)
    send_rows([product], out_ref, spaced_ref)


def attend_kernel(
    row_groups,
    turn_ref,
    key_scale_ref,
    value_scale_ref,
    sums_ref,
    keys_ref,
    values_ref,
    blocks_ref,
    result_ref,
    factor_ref,
):
    capacity = keys_ref.shape[0]
    scale_blocks = key_scale_ref.shape[1]
    block = capacity // scale_blocks
    inv_root = 1.0 / math.sqrt(HEAD_SIZE)
    per_group = GROUP + 2
    cosine, sine = turn_ref[0:1, :], turn_ref[1:2, :]
    length = turn_ref[2:3, 0:1].astype(jnp.int32)
    spans = [slice(b * block, (b + 1) * block) for b in range(scale_blocks)]

    def rotate(wide):
        return (wide * cosine + pltpu.roll(wide, HEAD_SIZE // 2, 1) * sine).astype(jnp.bfloat16)

    def summed(first, count):
        total = sums_ref[first : first + count, :]
        for i in range(1, row_groups):
            start = i * KEY_VALUE_HEADS * per_group + first
            total = total + sums_ref[start : start + count, :]
        return total.astype(jnp.bfloat16).astype(jnp.float32)

    shape = (KEY_VALUE_HEADS, block)
    for b, span in enumerate(spans):
        factor_ref[0:KEY_VALUE_HEADS, span] = jnp.broadcast_to(
            key_scale_ref[:, b : b + 1] * inv_root, shape
        )
        factor_ref[KEY_VALUE_HEADS:, span] = jnp.broadcast_to(value_scale_ref[:, b : b + 1], shape)

    def factors(row, span):
        return jnp.broadcast_to(factor_ref[row : row + 1, span], (GROUP, block))

    positions = lax.broadcasted_iota(jnp.int32, (GROUP, block), 1)

    def score(g):
        query = rotate(summed(g * per_group, GROUP))
        new_key = rotate(summed(g * per_group + GROUP, 1))
        own = (
            jnp.sum(
                query.astype(jnp.float32) * new_key.astype(jnp.float32), axis=1, keepdims=True
            )
            * inv_root
        )
        raw = lax.dot_general(
            query,
            keys_ref[:, g * HEAD_SIZE : (g + 1) * HEAD_SIZE],
            (((1,), (1,)), ((), ())),
            preferred_element_type=jnp.float32,
        )
        return raw, own

    def weigh(g, raw, own):
        scores = [
            jnp.where(
                positions < length - b * block, raw[:, span] * factors(g, span), MASKED_SCORE
            )
            for b, span in enumerate(spans)
        ]
        peak = jnp.maximum(
            jnp.max(functools.reduce(jnp.maximum, scores), axis=1, keepdims=True), own
        )
        probs = [jnp.exp(part - peak) for part in scores]
        own_prob = jnp.exp(own - peak)
        total = jnp.sum(functools.reduce(jnp.add, probs), axis=1, keepdims=True) + own_prob
        weighted = [
            prob * factors(KEY_VALUE_HEADS + g, span) for prob, span in zip(probs, spans)
        ]
        new_value = summed(g * per_group + GROUP + 1, 1)
        own_part = own_prob.astype(jnp.bfloat16).astype(jnp.float32) * new_value
        return weighted, own_part, total

    def finish(g, weighed):
        lhs = jnp.concatenate(
            [jnp.concatenate(parts, axis=0) for parts in zip(weighed[0][0], weighed[1][0])], axis=1
        )
        both = jnp.dot(
            lhs.astype(jnp.bfloat16),
            values_ref[:, g * HEAD_SIZE : (g + 2) * HEAD_SIZE],
            preferred_element_type=jnp.float32,
        )
        for n, (_, own_part, total) in enumerate(weighed):
            part = both[n * GROUP : (n + 1) * GROUP, n * HEAD_SIZE : (n + 1) * HEAD_SIZE]
            result_ref[(g + n) * GROUP : (g + n + 1) * GROUP, :] = (part + own_part) / total

    ahead = [score(0), score(1)]
    for g in range(0, KEY_VALUE_HEADS, 2):
        now = ahead
        if g + 2 < KEY_VALUE_HEADS:
            ahead = [score(g + 2), score(g + 3)]
        finish(g, [weigh(g + n, *now[n]) for n in range(2)])
    spread_blocks(result_ref[...].astype(jnp.bfloat16), row_groups, blocks_ref)


def body(
    hidden_in,
    norm_gain,
    w_query,
    key_weight,
    value_weight,
    w_output,
    key_cache_units,
    value_cache_units,
    key_scale,
    value_block_scale,
    lengths,
):
    row_groups, column_groups = lax.axis_size("gx"), lax.axis_size("gy")
    devices = row_groups * column_groups
    width = hidden_in.shape[1]
    slice_rows = width // row_groups // LANES
    query_cols, key_cols = w_query.shape[1], key_weight.shape[1]
    out_cols = w_output.shape[1]
    blocks_type = jax.ShapeDtypeStruct((devices, slice_rows, LANES), jnp.bfloat16)

    turn_type = jax.ShapeDtypeStruct((8, HEAD_SIZE), jnp.float32)
    table = pl.pallas_call(
        freqs_kernel,
        out_shape=turn_type,
        out_specs=VMEM,
        compiler_params=PARAMS,
        cost_estimate=COST,
    )()
    lengths, table = lax.optimization_barrier((lengths, table))
    turn = pl.pallas_call(
        turn_kernel,
        out_shape=turn_type,
        in_specs=[SMEM, VMEM],
        out_specs=VMEM,
        compiler_params=PARAMS,
    )(lengths, table)
    blocks = pl.pallas_call(
        functools.partial(norm_kernel, row_groups),
        out_shape=blocks_type,
        in_specs=[VMEM] * 3,
        out_specs=VMEM,
        scratch_shapes=[pltpu.VMEM((width // LANES, LANES), jnp.float32)],
        compiler_params=PARAMS,
        cost_estimate=COST,
    )(turn, in_vmem(hidden_in), in_vmem(norm_gain.reshape(-1, LANES)))

    sent_rows = (query_cols + 2 * key_cols) // LANES
    partial = pl.pallas_call(
        project_kernel,
        out_shape=jax.ShapeDtypeStruct((devices * sent_rows, LANES), jnp.float32),
        in_specs=[VMEM] * 4,
        out_specs=VMEM,
        scratch_shapes=[spaced(devices, sent_rows)],
        compiler_params=PARAMS,
        cost_estimate=COST,
    )(exchange(blocks), in_vmem(w_query), in_vmem(key_weight), in_vmem(value_weight))
    sums = exchange(partial.reshape(devices, sent_rows, 1, LANES))
    if key_cols != HEAD_SIZE:
        sums = sums.reshape(row_groups, column_groups, sent_rows * LANES)
        sums = jnp.concatenate(
            [
                part.reshape(row_groups, KEY_VALUE_HEADS, -1, HEAD_SIZE)
                for part in jnp.split(sums, (query_cols, query_cols + key_cols), axis=2)
            ],
            axis=2,
        )
    sums = sums.reshape(-1, LANES)

    attended = pl.pallas_call(
        functools.partial(attend_kernel, row_groups),
        out_shape=blocks_type,
        in_specs=[VMEM] * 6,
        out_specs=VMEM,
        scratch_shapes=[
            pltpu.VMEM((HQ, HEAD_SIZE), jnp.float32),
            pltpu.VMEM((2 * KEY_VALUE_HEADS, key_cache_units.shape[1]), jnp.float32),
        ],
        compiler_params=PARAMS,
        cost_estimate=COST,
    )(
        turn,
        key_scale[0].T,
        value_block_scale[0].T,
        sums,
        in_vmem(key_cache_units[0]),
        in_vmem(value_cache_units[0]),
    )

    out_rows = out_cols // LANES
    partial = pl.pallas_call(
        output_kernel,
        out_shape=jax.ShapeDtypeStruct((devices * out_rows, LANES), jnp.bfloat16),
        in_specs=[VMEM] * 2,
        out_specs=VMEM,
        scratch_shapes=[spaced(devices, out_rows)],
        compiler_params=PARAMS,
        cost_estimate=COST,
    )(exchange(attended), in_vmem(w_output))
    update = exchange(partial.reshape(devices, out_rows, LANES)).astype(jnp.float32)
    update = jnp.sum(update.reshape(row_groups, column_groups * out_rows, LANES), axis=0)
    return (hidden_in.astype(jnp.float32) + update.reshape(1, width)).astype(jnp.bfloat16)


def solution(mesh):
    placed = (
        P(("gx", "gy"), None),
        P(),
        P("gx", "gy"),
        P("gx", "gy"),
        P("gx", "gy"),
        P("gx", "gy"),
        P(("gx", "gy"), None, None),
        P(("gx", "gy"), None, None),
        P(("gx", "gy"), None, None),
        P(("gx", "gy"), None, None),
        P(("gx", "gy")),
    )
    return jax.shard_map(
        body, mesh=mesh, in_specs=placed, out_specs=P(("gx", "gy"), None), check_vma=False
    )
```

```python
import functools
import math

import jax
import jax.numpy as jnp
from jax import lax
from jax.experimental import pallas as pl
from jax.experimental.pallas import tpu as pltpu
from jax.sharding import PartitionSpec as P

HQ = 64
KEY_VALUE_HEADS = 8
HEAD_SIZE = 128
GROUP = HQ // KEY_VALUE_HEADS

ROPE_BASE = 500000.0
NORM_EPS = 1e-05
MASKED_SCORE = -1e30

LANES = 128
VMEM = pl.BlockSpec(memory_space=pltpu.VMEM)
SMEM = pl.BlockSpec(memory_space=pltpu.SMEM)
PARAMS = pltpu.CompilerParams(vmem_limit_bytes=4 * 1024 * 1024)
COST = pl.CostEstimate(flops=20_000_000_000, transcendentals=0, bytes_accessed=0)


def exchange(blocks):
    return lax.all_to_all(blocks, ("gx", "gy"), split_axis=0, concat_axis=0, tiled=True)


def in_vmem(array):
    return pltpu.with_memory_space_constraint(array, pltpu.VMEM)


def freqs_kernel(table_ref):
    half = HEAD_SIZE // 2
    lanes = lax.broadcasted_iota(jnp.int32, (1, HEAD_SIZE), 1)
    places = jnp.where(lanes < half, lanes, lanes - half)
    freqs = jnp.zeros((1, HEAD_SIZE), jnp.float32)
    for i in range(half):
        freqs = jnp.where(places == i, ROPE_BASE ** (-2.0 * i / HEAD_SIZE), freqs)
    table_ref[0:1, :] = freqs
    table_ref[1:2, :] = jnp.where(lanes < half, -1.0, 1.0)


def turn_kernel(length_ref, table_ref, turn_ref):
    length = length_ref[0].astype(jnp.float32)
    angles = length * table_ref[0:1, :]
    turn_ref[0:1, :] = jnp.cos(angles)
    turn_ref[1:2, :] = jnp.sin(angles) * table_ref[1:2, :]
    turn_ref[2:3, :] = jnp.full((1, HEAD_SIZE), length)


def norm_kernel(row_groups, turn_ref, hidden_ref, gain_ref, blocks_ref):
    rows = gain_ref.shape[0]
    wide = hidden_ref[...].astype(jnp.float32).reshape(rows, LANES)
    variance = jnp.sum(wide * wide, keepdims=True) * (1.0 / (rows * LANES))
    normed = (wide * lax.rsqrt(variance + NORM_EPS) * gain_ref[...]).astype(jnp.bfloat16)
    spread_blocks(normed, row_groups, blocks_ref)


def spread_blocks(rows, row_groups, blocks_ref):
    per_block = rows.shape[0] // row_groups
    column_groups = blocks_ref.shape[0] // row_groups
    for i in range(row_groups):
        part = rows[i * per_block : (i + 1) * per_block]
        for j in range(column_groups):
            blocks_ref[i * column_groups + j] = part


def flat_rows(blocks_ref):
    return jnp.concatenate([blocks_ref[:, k, :] for k in range(blocks_ref.shape[1])], axis=1)


def spaced(requests, count):
    return pltpu.VMEM(((requests + 1) * count, LANES), jnp.float32)


def send_rows(products, out_ref, spaced_ref):
    requests = products[0].shape[0]
    count = out_ref.shape[0] // requests
    parts = [
        product[:, start : start + LANES]
        for product in products
        for start in range(0, product.shape[1], LANES)
    ]
    for n, part in enumerate(parts):
        spaced_ref[pl.ds(n, requests, stride=count), :] = part
    out_ref[...] = spaced_ref[: requests * count, :].astype(out_ref.dtype)


def project_kernel(blocks_ref, w_query_ref, key_ref, value_ref, out_ref, spaced_ref):
    rows = flat_rows(blocks_ref)
    products = [
        jnp.dot(rows, ref[...], preferred_element_type=jnp.float32)
        for ref in (w_query_ref, key_ref, value_ref)
    ]
    if products[1].shape[1] % LANES:
        products[1:] = [jnp.concatenate(products[1:], axis=1)]
    send_rows(products, out_ref, spaced_ref)


def output_kernel(blocks_ref, weight_ref, out_ref, spaced_ref):
    rows = flat_rows(blocks_ref)
    product = jnp.dot(rows, weight_ref[...], preferred_element_type=jnp.float32)
    send_rows([product], out_ref, spaced_ref)


def attend_kernel(
    row_groups,
    turn_ref,
    key_scale_ref,
    value_scale_ref,
    sums_ref,
    keys_ref,
    values_ref,
    blocks_ref,
    result_ref,
    factor_ref,
):
    capacity = keys_ref.shape[0]
    scale_blocks = key_scale_ref.shape[1]
    block = capacity // scale_blocks
    inv_root = 1.0 / math.sqrt(HEAD_SIZE)
    per_group = GROUP + 2
    cosine, sine = turn_ref[0:1, :], turn_ref[1:2, :]
    length = turn_ref[2:3, 0:1].astype(jnp.int32)
    spans = [slice(b * block, (b + 1) * block) for b in range(scale_blocks)]

    def rotate(wide):
        return (wide * cosine + pltpu.roll(wide, HEAD_SIZE // 2, 1) * sine).astype(jnp.bfloat16)

    def summed(first, count):
        total = sums_ref[first : first + count, :]
        for i in range(1, row_groups):
            start = i * KEY_VALUE_HEADS * per_group + first
            total = total + sums_ref[start : start + count, :]
        return total.astype(jnp.bfloat16).astype(jnp.float32)

    shape = (KEY_VALUE_HEADS, block)
    for b, span in enumerate(spans):
        factor_ref[0:KEY_VALUE_HEADS, span] = jnp.broadcast_to(
            key_scale_ref[:, b : b + 1] * inv_root, shape
        )
        factor_ref[KEY_VALUE_HEADS:, span] = jnp.broadcast_to(value_scale_ref[:, b : b + 1], shape)

    def factors(row, span):
        return jnp.broadcast_to(factor_ref[row : row + 1, span], (GROUP, block))

    positions = lax.broadcasted_iota(jnp.int32, (GROUP, block), 1)

    def score(g):
        query = rotate(summed(g * per_group, GROUP))
        new_key = rotate(summed(g * per_group + GROUP, 1))
        own = (
            jnp.sum(
                query.astype(jnp.float32) * new_key.astype(jnp.float32), axis=1, keepdims=True
            )
            * inv_root
        )
        raw = lax.dot_general(
            query,
            keys_ref[:, g * HEAD_SIZE : (g + 1) * HEAD_SIZE],
            (((1,), (1,)), ((), ())),
            preferred_element_type=jnp.float32,
        )
        return raw, own

    def weigh(g, raw, own):
        scores = [
            jnp.where(
                positions < length - b * block, raw[:, span] * factors(g, span), MASKED_SCORE
            )
            for b, span in enumerate(spans)
        ]
        peak = jnp.maximum(
            jnp.max(functools.reduce(jnp.maximum, scores), axis=1, keepdims=True), own
        )
        probs = [jnp.exp(part - peak) for part in scores]
        own_prob = jnp.exp(own - peak)
        total = jnp.sum(functools.reduce(jnp.add, probs), axis=1, keepdims=True) + own_prob
        weighted = [
            prob * factors(KEY_VALUE_HEADS + g, span) for prob, span in zip(probs, spans)
        ]
        new_value = summed(g * per_group + GROUP + 1, 1)
        own_part = own_prob.astype(jnp.bfloat16).astype(jnp.float32) * new_value
        return weighted, own_part, total

    def finish(g, weighed):
        lhs = jnp.concatenate(
            [jnp.concatenate(parts, axis=0) for parts in zip(weighed[0][0], weighed[1][0])], axis=1
        )
        both = jnp.dot(
            lhs.astype(jnp.bfloat16),
            values_ref[:, g * HEAD_SIZE : (g + 2) * HEAD_SIZE],
            preferred_element_type=jnp.float32,
        )
        for n, (_, own_part, total) in enumerate(weighed):
            part = both[n * GROUP : (n + 1) * GROUP, n * HEAD_SIZE : (n + 1) * HEAD_SIZE]
            result_ref[(g + n) * GROUP : (g + n + 1) * GROUP, :] = (part + own_part) / total

    ahead = [score(0), score(1)]
    for g in range(0, KEY_VALUE_HEADS, 2):
        now = ahead
        if g + 2 < KEY_VALUE_HEADS:
            ahead = [score(g + 2), score(g + 3)]
        finish(g, [weigh(g + n, *now[n]) for n in range(2)])
    spread_blocks(result_ref[...].astype(jnp.bfloat16), row_groups, blocks_ref)


def body(
    hidden_in,
    norm_gain,
    w_query,
    key_weight,
    value_weight,
    w_output,
    key_cache_units,
    value_cache_units,
    key_scale,
    value_block_scale,
    lengths,
):
    row_groups, column_groups = lax.axis_size("gx"), lax.axis_size("gy")
    devices = row_groups * column_groups
    width = hidden_in.shape[1]
    slice_rows = width // row_groups // LANES
    query_cols, key_cols = w_query.shape[1], key_weight.shape[1]
    out_cols = w_output.shape[1]
    blocks_type = jax.ShapeDtypeStruct((devices, slice_rows, LANES), jnp.bfloat16)

    turn_type = jax.ShapeDtypeStruct((8, HEAD_SIZE), jnp.float32)
    table = pl.pallas_call(
        freqs_kernel,
        out_shape=turn_type,
        out_specs=VMEM,
        compiler_params=PARAMS,
        cost_estimate=COST,
    )()
    lengths, table = lax.optimization_barrier((lengths, table))
    turn = pl.pallas_call(
        turn_kernel,
        out_shape=turn_type,
        in_specs=[SMEM, VMEM],
        out_specs=VMEM,
        compiler_params=PARAMS,
    )(lengths, table)
    blocks = pl.pallas_call(
        functools.partial(norm_kernel, row_groups),
        out_shape=blocks_type,
        in_specs=[VMEM] * 3,
        out_specs=VMEM,
        compiler_params=PARAMS,
        cost_estimate=COST,
    )(turn, in_vmem(hidden_in), in_vmem(norm_gain.reshape(-1, LANES)))

    sent_rows = (query_cols + 2 * key_cols) // LANES
    partial = pl.pallas_call(
        project_kernel,
        out_shape=jax.ShapeDtypeStruct((devices * sent_rows, LANES), jnp.float32),
        in_specs=[VMEM] * 4,
        out_specs=VMEM,
        scratch_shapes=[spaced(devices, sent_rows)],
        compiler_params=PARAMS,
        cost_estimate=COST,
    )(exchange(blocks), in_vmem(w_query), in_vmem(key_weight), in_vmem(value_weight))
    pair = 2 if sent_rows % 2 == 0 else 1
    sums = exchange(partial.reshape(devices, sent_rows // pair, pair, LANES))
    if key_cols != HEAD_SIZE:
        sums = sums.reshape(row_groups, column_groups, sent_rows * LANES)
        sums = jnp.concatenate(
            [
                part.reshape(row_groups, KEY_VALUE_HEADS, -1, HEAD_SIZE)
                for part in jnp.split(sums, (query_cols, query_cols + key_cols), axis=2)
            ],
            axis=2,
        )
    sums = sums.reshape(-1, LANES)

    attended = pl.pallas_call(
        functools.partial(attend_kernel, row_groups),
        out_shape=blocks_type,
        in_specs=[VMEM] * 6,
        out_specs=VMEM,
        scratch_shapes=[
            pltpu.VMEM((HQ, HEAD_SIZE), jnp.float32),
            pltpu.VMEM((2 * KEY_VALUE_HEADS, key_cache_units.shape[1]), jnp.float32),
        ],
        compiler_params=PARAMS,
        cost_estimate=COST,
    )(
        turn,
        key_scale[0].T,
        value_block_scale[0].T,
        sums,
        in_vmem(key_cache_units[0]),
        in_vmem(value_cache_units[0]),
    )

    out_rows = out_cols // LANES
    partial = pl.pallas_call(
        output_kernel,
        out_shape=jax.ShapeDtypeStruct((devices * out_rows, LANES), jnp.bfloat16),
        in_specs=[VMEM] * 2,
        out_specs=VMEM,
        scratch_shapes=[spaced(devices, out_rows)],
        compiler_params=PARAMS,
        cost_estimate=COST,
    )(exchange(attended), in_vmem(w_output))
    update = exchange(partial.reshape(devices, out_rows, LANES)).astype(jnp.float32)
    update = jnp.sum(update.reshape(row_groups, column_groups * out_rows, LANES), axis=0)
    return (hidden_in.astype(jnp.float32) + update.reshape(1, width)).astype(jnp.bfloat16)


def solution(mesh):
    placed = (
        P(("gx", "gy"), None),
        P(),
        P("gx", "gy"),
        P("gx", "gy"),
        P("gx", "gy"),
        P("gx", "gy"),
        P(("gx", "gy"), None, None),
        P(("gx", "gy"), None, None),
        P(("gx", "gy"), None, None),
        P(("gx", "gy"), None, None),
        P(("gx", "gy")),
    )
    return jax.shard_map(
        body, mesh=mesh, in_specs=placed, out_specs=P(("gx", "gy"), None), check_vma=False
    )
```
